32 devices in a mesh: seq: 8 (over y, x, core), blk: 4 (over z).
Axes of the slice: x: 2, y: 2, z: 4, core: 2. Of those that a mesh axis runs over, the one named last changes fastest.
Arguments:
- alphas: float32 [2, 512, 32768], P(None, 'seq', 'blk'), may hold values from 0.05 to 1
- betas: float32 [2, 512, 65536], P(None, 'seq', 'blk'), may hold values from 0.05 to 1
- token_ids: int32 [2, 512], P(None, 'seq'), may hold values from 0 to 31
- emission: float32 [32, 65536], P(None, 'blk'), may hold values from 0.05 to 1
- left_blocks: float32 [64, 128, 512], P('blk'), may hold values from 0.000390625 to 0.00390625
- right_blocks: float32 [128, 64, 512], P('blk', 'seq'), may hold values from 0.003125 to 0.03125
Outputs:
- left_grad: float32 [64, 128, 512], P('blk', 'seq')
- right_grad: float32 [128, 64, 512], P('blk', 'seq')
The draws below stay inside these ranges and needn't reach their ends.
All inputs are finite; a program needn't handle non-finite values.
Results may differ from the reference program's by a relative error of at most 0.0001.
Values sent between devices are 32-bit elements; how exact they have to be, the bound alone decides.
A program may use at most 128 MiB of HBM per device.

```python
import math
import jax
import jax.numpy as jnp
from jax import lax

BS = 512
NB = 512
IW = 64
KW = 128
SEQ_DEV = 64
UNIQ = 32
SIN = 32768
SW = 65536
SEQS = 512
N_SEQ = 8


def plant(entries, rng, least, largest):
    dims = entries.shape
    place = [jax.random.randint(jax.random.fold_in(rng, axis), (), 0, dims[axis]) for axis in range(len(dims))]
    entries = entries.at[tuple(place)].set(least)
    longest = dims.index(max(dims))
    place[longest] = (place[longest] + 1) % dims[longest]
    return entries.at[tuple(place)].set(largest)


def shard_levels(stream_key, extent, pieces, smallest, high):
    level = 1.0
    for position, parts in pieces:
        steps = jax.random.uniform(jax.random.fold_in(jax.random.fold_in(stream_key, 6), position), (parts,), jnp.float32, smallest / len(pieces), high / len(pieces))
        level = level * jnp.repeat(jnp.exp(steps), extent[position] // parts).reshape((-1,) + (1,) * (len(extent) - 1 - position))
    return level


def setup_inputs(seed: int = 0) -> dict:
    arg_keys = jax.random.split(jax.random.key(seed), 7)
    alphas = jnp.clip(jnp.exp(math.log(1.0) - 2.9957323 * jax.random.uniform(arg_keys[0], (2, SEQS, SIN), jnp.float32) ** shard_levels(arg_keys[0], (2, SEQS, SIN), ((1, 8), (2, 4)), -0.2, 0.2)), 0.05, 1.0)
    betas = jnp.clip(jnp.exp(math.log(1.0) - 2.9957323 * jax.random.uniform(arg_keys[1], (2, SEQS, SW), jnp.float32) ** shard_levels(arg_keys[1], (2, SEQS, SW), ((1, 8), (2, 4)), -0.2, 0.2)), 0.05, 1.0)
    token_ids = plant(jax.random.randint(arg_keys[2], (2, SEQS), 0, UNIQ), jax.random.fold_in(arg_keys[2], 1), 0, UNIQ - 1).astype(jnp.int32)
    emission = jnp.clip(jnp.exp(math.log(1.0) - 2.9957323 * jax.random.uniform(arg_keys[3], (UNIQ, SW), jnp.float32) ** shard_levels(arg_keys[3], (UNIQ, SW), ((1, 4),), -0.2, 0.2)), 0.05, 1.0)
    left_blocks = jnp.clip(jnp.exp(math.log(0.00390625) - 2.3025851 * jax.random.uniform(arg_keys[4], (IW, KW, BS), jnp.float32) ** shard_levels(arg_keys[4], (IW, KW, BS), ((0, 4),), -0.2, 0.2)), 0.000390625, 0.00390625)
    right_blocks = jnp.clip(jnp.exp(math.log(0.03125) - 2.3025851 * jax.random.uniform(arg_keys[5], (KW, IW, NB), jnp.float32) ** shard_levels(arg_keys[5], (KW, IW, NB), ((0, 4), (1, 8)), -0.2, 0.2)), 0.003125, 0.03125)
    return {"alphas": alphas, "betas": betas, "token_ids": token_ids, "emission": emission, "left_blocks": left_blocks, "right_blocks": right_blocks}


def reference(alphas, betas, token_ids, emission, left_blocks, right_blocks):
    seqs = alphas.shape[1]
    scale = (KW * NB) / (2.0 * seqs)
    count = 2 * N_SEQ
    alpha_blocks = alphas.reshape(count, SEQ_DEV, IW * BS)
    beta_blocks = betas.reshape(count, SEQ_DEV, KW * NB)
    id_blocks = token_ids.reshape(count, SEQ_DEV)
    high = lax.Precision.HIGHEST

    def visit(carry, item):
        grad_left, grad_right = carry
        a_flat, b_flat, ids = item
        a_rows = a_flat.reshape(SEQ_DEV, IW, BS)
        mixed = jnp.einsum('bij,ikj->bik', a_rows, left_blocks, precision=high)
        outputs = jnp.einsum('bik,kim->bkm', mixed, right_blocks, precision=high)
        rows = jnp.take(emission, ids, axis=0)
        signal = (rows * b_flat).reshape(SEQ_DEV, KW, NB)
        total = jnp.sum(outputs * signal, axis=(1, 2))
        weighted = signal * (scale / total)[:, None, None]
        grad_right = grad_right + jnp.einsum('bik,bkm->kim', mixed, weighted, precision=high)
        back = jnp.einsum('kim,bkm->bik', right_blocks, weighted, precision=high)
        grad_left = grad_left + jnp.einsum('bij,bik->ikj', a_rows, back, precision=high)
        return (grad_left, grad_right), None

    start = (jnp.zeros((IW, KW, BS), jnp.float32), jnp.zeros((KW, IW, NB), jnp.float32))
    (grad_left, grad_right), _ = lax.scan(visit, start, (alpha_blocks, beta_blocks, id_blocks))
    return grad_left, grad_right
```

```python
import jax
import jax.numpy as jnp
from jax import lax
from jax.sharding import PartitionSpec as P


def local(alphas, betas, token_ids, emission, left_blocks, right_blocks):
    high = lax.Precision.HIGH
    seq_dev = alphas.shape[1]
    count = 2 * seq_dev
    blocks_here, window, width = left_blocks.shape
    local_k, rows_right, nblocks = right_blocks.shape
    scale = window * nblocks / (2.0 * seq_dev * lax.axis_size("seq"))

    right_full = lax.all_gather(right_blocks, "seq", axis=1, tiled=True)
    a_rows = alphas.reshape(count, blocks_here, width)
    mixed = jnp.einsum("ikj,bij->kib", left_blocks, a_rows, precision=high)
    spread = lax.all_to_all(mixed, "blk", split_axis=0, concat_axis=1, tiled=True)
    rows = jnp.take(emission, token_ids.reshape(count), axis=0)
    signal = (rows * betas.reshape(count, -1)).reshape(count, local_k, nblocks)
    back = jnp.einsum("kim,bkm->kib", right_full, signal, precision=high)
    total = lax.psum(jnp.sum(spread * back, axis=(0, 1)), "blk")
    weight = scale / total
    returned = lax.all_to_all(back, "blk", split_axis=1, concat_axis=0, tiled=True)
    right_sum = jnp.einsum("kib,bkm->ikm", spread * weight, signal, precision=high)
    right_rows = lax.psum_scatter(right_sum, "seq", scatter_dimension=0, tiled=True)
    left_sum = jnp.einsum("kib,bij->kij", returned * weight, a_rows, precision=high)
    left_rows = lax.psum_scatter(left_sum, "seq", scatter_dimension=0, tiled=True)
    return (left_rows.transpose(1, 0, 2), right_rows.transpose(1, 0, 2))


def solution(mesh):
    placed = (
        P(None, "seq", "blk"),
        P(None, "seq", "blk"),
        P(None, "seq"),
        P(None, "blk"),
        P("blk", None, None),
        P("blk", "seq", None),
    )
    return jax.shard_map(
        local,
        mesh=mesh,
        in_specs=placed,
        out_specs=(P("blk", "seq", None), P("blk", "seq", None)),
        check_vma=False,
    )
```

```python
import functools
import jax
import jax.numpy as jnp
from jax import lax
from jax.experimental import pallas as pl
from jax.experimental.pallas import tpu as pltpu
from jax.sharding import PartitionSpec as P

F32 = jnp.float32
BF16 = jnp.bfloat16
CHIPS = 4
CHUNKS = 4


def halves(x):
    top = x.astype(BF16)
    rest = (x - top.astype(F32)).astype(BF16)
    return jnp.concatenate([top, rest], axis=0)


def nt(a, b):
    return lax.dot_general(a, b, (((1,), (1,)), ((), ())), preferred_element_type=F32)


def kernel(
    nz, scale, a_hbm, b_hbm, hot_ref, e_hbm, l_hbm, r_hbm, left_out, right_out,
    a32, b32, e32, l32, a16, g16, rf, us, ur, hs, hr, pr, pl_, rx0r, rx0l, rx1r, rx1l, cs, cr,
    load_a, load_l, load_b, load_e, load_r, own_u, own_h,
    ag_s, ag_r, fw_s, fw_r, u_s, u_r, h_s, h_r, c_s, c_r, s0_s, s0_r, s1_s, s1_r,
):
    seq = lax.axis_index("seq")
    z = lax.axis_index("blk")
    core, chip = seq % 2, seq // 2
    x, y = chip % 2, chip // 2
    sibling = 2 * chip + 1 - core
    chips = (2 * y + 1 - x, 2 * (1 - y) + x, 2 * (1 - y) + 1 - x)
    peers = tuple(2 * other + core for other in chips)
    blocks_here, window, width = l32.shape
    local_k, nblocks = g16.shape[0], g16.shape[2]
    count = a16.shape[1] // 2
    seq_dev = count // 2
    inputs = nz * blocks_here
    part_i, part_k = blocks_here // CHUNKS, local_k // CHUNKS
    rows_z = blocks_here * local_k
    rows_c = part_i * local_k

    loads_a, loads_l, loads_b, loads_e = [], [], [], []
    for n in range(CHUNKS):
        cols = pl.ds(n * part_i * width, part_i * width)
        loads_a.append(pltpu.make_async_copy(a_hbm.at[:, :, cols], a32.at[:, :, cols], load_a.at[n]))
        some = pl.ds(n * part_i, part_i)
        loads_l.append(pltpu.make_async_copy(l_hbm.at[some], l32.at[some], load_l.at[n]))
        cols = pl.ds(n * part_k * nblocks, part_k * nblocks)
        loads_b.append(pltpu.make_async_copy(b_hbm.at[:, :, cols], b32.at[:, :, cols], load_b.at[n]))
        loads_e.append(pltpu.make_async_copy(e_hbm.at[:, cols], e32.at[:, cols], load_e.at[n]))
    load_own = pltpu.make_async_copy(r_hbm, rf.at[seq], load_r)
    load_own.start()
    for n in range(CHUNKS):
        loads_l[n].start()
        loads_a[n].start()
    for n in range(CHUNKS):
        loads_e[n].start()
        loads_b[n].start()

    barrier = pltpu.get_barrier_semaphore()
    for other in (sibling,) + peers:
        pl.semaphore_signal(barrier, inc=1, device_id={"seq": other}, device_id_type=pl.DeviceIdType.MESH)
    for d in range(1, nz):
        pl.semaphore_signal(barrier, inc=1, device_id={"blk": (z + d) % nz}, device_id_type=pl.DeviceIdType.MESH)
    pl.semaphore_wait(barrier, 4 + nz - 1)

    def to_seq(src, dst, send, recv, other):
        return pltpu.make_async_remote_copy(
            src_ref=src, dst_ref=dst, send_sem=send, recv_sem=recv,
            device_id={"seq": other}, device_id_type=pl.DeviceIdType.MESH,
        )

    def to_blk(src, dst, send, recv, other):
        return pltpu.make_async_remote_copy(
            src_ref=src, dst_ref=dst, send_sem=send, recv_sem=recv,
            device_id={"blk": other}, device_id_type=pl.DeviceIdType.MESH,
        )

    gathers = [to_seq(r_hbm, rf.at[seq], ag_s.at[n], ag_r.at[n], other) for n, other in enumerate(peers + (sibling,))]
    for copy in gathers:
        copy.start()

    def u_block(i, _):
        cols = pl.ds(pl.multiple_of(i * width, width), width)
        a = halves(jnp.concatenate([a32[0, :, cols], a32[1, :, cols]], axis=0))
        a16[i] = a
        both = nt(halves(l32[i]), a)
        u = both[:window, :count] + both[:window, count:] + both[window:, :count]
        for dz in range(nz):
            us[pl.ds(dz * rows_z + i * local_k, local_k), :] = u[dz * local_k:(dz + 1) * local_k]
        return 0

    for n in range(CHUNKS):
        loads_l[n].wait()
        loads_a[n].wait()
        lax.fori_loop(n * part_i, (n + 1) * part_i, u_block, 0)
    u_own = pltpu.make_async_copy(us.at[pl.ds(z * rows_z, rows_z)], ur.at[pl.ds(z * rows_z, rows_z)], own_u)
    u_own.start()
    u_sends = []
    for d in range(1, nz):
        other = (z + d) % nz
        copy = to_blk(
            us.at[pl.ds(other * rows_z, rows_z)], ur.at[pl.ds(z * rows_z, rows_z)], u_s.at[d - 1], u_r.at[d - 1], other
        )
        copy.start()
        u_sends.append(copy)

    hot = hot_ref[...]

    def g_block(k, _):
        cols = pl.ds(pl.multiple_of(k * nblocks, nblocks), nblocks)
        e = e32[:, cols]
        e1 = e.astype(BF16)
        rest = e - e1.astype(F32)
        e2 = rest.astype(BF16)
        e3 = (rest - e2.astype(F32)).astype(BF16)
        picked = jnp.dot(hot, jnp.concatenate([e1, e2, e3], axis=0), preferred_element_type=F32)
        b = jnp.concatenate([b32[0, :, cols], b32[1, :, cols]], axis=0)
        g16[k] = halves(picked * b)
        return 0

    for n in range(CHUNKS):
        loads_e[n].wait()
        loads_b[n].wait()
        lax.fori_loop(n * part_k, (n + 1) * part_k, g_block, 0)

    load_own.wait()
    forwards = []
    for n, other in enumerate(peers):
        gathers[n].wait_recv()
        slot = rf.at[other]
        copy = to_seq(slot, slot, fw_s.at[n], fw_r.at[n], sibling)
        copy.start()
        forwards.append(copy)
    gathers[3].wait_recv()
    for copy in forwards:
        copy.wait_recv()

    def h_block(k, _):
        r = halves(jnp.concatenate([rf[s, k] for s in range(2 * CHIPS)], axis=0))
        both = nt(r, g16[k])
        h = both[:inputs, :count] + both[:inputs, count:] + both[inputs:, :count]
        hs[pl.ds(k, inputs, stride=local_k), :] = h
        return 0

    lax.fori_loop(0, local_k, h_block, 0)

    u_own.wait()
    for copy in u_sends:
        copy.wait_recv()
    step = 64

    def c_block(n, acc):
        rows = pl.ds(pl.multiple_of(n * step, step), step)
        return acc + jnp.sum((ur[rows, :] * hs[rows, :]).reshape(step // 8, 8, count), axis=0)

    acc = lax.fori_loop(0, nz * rows_z // step, c_block, jnp.zeros((8, count), F32))
    cs[...] = acc
    c_sends = []
    for d in range(1, nz):
        copy = to_blk(cs, cr.at[d - 1], c_s.at[d - 1], c_r.at[d - 1], (z + d) % nz)
        copy.start()
        c_sends.append(copy)
    h_own = pltpu.make_async_copy(hs.at[pl.ds(z * rows_z, rows_z)], hr.at[pl.ds(z * rows_z, rows_z)], own_h)
    h_own.start()
    h_sends = []
    for n in range(CHUNKS):
        for d in range(1, nz):
            other = (z + d) % nz
            copy = to_blk(
                hs.at[pl.ds(other * rows_z + n * rows_c, rows_c)],
                hr.at[pl.ds(z * rows_z + n * rows_c, rows_c)],
                h_s.at[n, d - 1], h_r.at[n, d - 1], other,
            )
            copy.start()
            h_sends.append(copy)
    total = acc
    for n, copy in enumerate(c_sends):
        copy.wait_recv()
        total = total + cr[n]
    weight = scale / jnp.sum(total, axis=0, keepdims=True)

    def right_part(n):
        def block(kk, _):
            k = n * part_k + kk
            u = halves(ur[pl.ds(k, inputs, stride=local_k), :] * weight)
            both = jnp.dot(jnp.concatenate([u, u], axis=1), g16[k], preferred_element_type=F32)
            grad = both[:inputs] + both[inputs:]
            rows = inputs // (2 * CHIPS)
            for s in range(2 * CHIPS):
                pr[n, s % 2, s // 2, kk] = grad[s * rows:(s + 1) * rows]
            return 0

        lax.fori_loop(0, part_k, block, 0)

    def left_part(n):
        def block(ii, _):
            i = n * part_i + ii
            h = jnp.concatenate(
                [hr[pl.ds(pl.multiple_of(sz * rows_z + i * local_k, local_k), local_k), :] for sz in range(nz)], axis=0
            )
            h = halves(h * weight)
            both = jnp.dot(jnp.concatenate([h, h], axis=1), a16[i], preferred_element_type=F32)
            grad = both[:window] + both[window:]
            rows = window // (2 * CHIPS)
            for s in range(2 * CHIPS):
                pl_[n, s % 2, s // 2, ii] = grad[s * rows:(s + 1) * rows]
            return 0

        lax.fori_loop(0, part_i, block, 0)

    firsts, seconds = {}, {}

    def first(m, mine, into, n):
        firsts[m] = to_seq(mine.at[n, 1 - core], into.at[n], s0_s.at[m], s0_r.at[m], sibling)
        firsts[m].start()

    def second(m, mine, got, into, n):
        firsts[m].wait_recv()

        def add(p, _):
            mine[n, core, p] = mine[n, core, p] + got[n, p]
            return 0

        lax.fori_loop(0, CHIPS, add, 0)
        seconds[m] = []
        for d, other in enumerate(chips):
            copy = to_seq(mine.at[n, core, other], into.at[d, n], s1_s.at[m, d], s1_r.at[m, d], peers[d])
            copy.start()
            seconds[m].append(copy)

    def last(m, mine, into, out, n, part):
        for copy in seconds[m]:
            copy.wait_recv()
        out[n * part:(n + 1) * part] = mine[n, core, chip] + into[0, n] + into[1, n] + into[2, n]

    for m in range(2 * CHUNKS):
        n = m % CHUNKS
        if m < CHUNKS:
            right_part(n)
            first(m, pr, rx0r, n)
        else:
            if n == 0:
                h_own.wait()
            for copy in h_sends[n * (nz - 1):(n + 1) * (nz - 1)]:
                copy.wait_recv()
            left_part(n)
            first(m, pl_, rx0l, n)
        if 1 <= m <= CHUNKS:
            second(m - 1, pr, rx0r, rx1r, m - 1)
        elif m > CHUNKS:
            second(m - 1, pl_, rx0l, rx1l, n - 1)
    second(2 * CHUNKS - 1, pl_, rx0l, rx1l, CHUNKS - 1)
    for n in range(CHUNKS):
        last(n, pr, rx1r, right_out, n, part_k)
    for n in range(CHUNKS):
        last(CHUNKS + n, pl_, rx1l, left_out, n, part_i)

    for copy in gathers + forwards + u_sends + c_sends + h_sends + list(firsts.values()):
        copy.wait_send()
    for copies in seconds.values():
        for copy in copies:
            copy.wait_send()


def fused(alphas, betas, token_ids, emission, left_blocks, right_blocks):
    nz = lax.axis_size("blk")
    seq_dev = alphas.shape[1]
    count = 2 * seq_dev
    blocks_here, window, width = left_blocks.shape
    local_k, rows_right, nblocks = right_blocks.shape
    rows_left = window // (2 * CHIPS)
    tokens = emission.shape[0]
    scale = window * nblocks / (2.0 * seq_dev * lax.axis_size("seq"))
    hot = (token_ids.reshape(count, 1) == (jnp.arange(3 * tokens, dtype=jnp.int32) % tokens)[None, :]).astype(BF16)
    part_i, part_k = blocks_here // CHUNKS, local_k // CHUNKS
    rows = nz * blocks_here * local_k
    dma = pltpu.SemaphoreType.DMA
    left_tile = (part_i, rows_left, width)
    right_tile = (part_k, rows_right, nblocks)
    scratch = [
        pltpu.VMEM(alphas.shape, F32),
        pltpu.VMEM(betas.shape, F32),
        pltpu.VMEM(emission.shape, F32),
        pltpu.VMEM(left_blocks.shape, F32),
        pltpu.VMEM((blocks_here, 2 * count, width), BF16),
        pltpu.VMEM((local_k, 2 * count, nblocks), BF16),
        pltpu.VMEM((2 * CHIPS,) + right_blocks.shape, F32),
        pltpu.VMEM((rows, count), F32),
        pltpu.VMEM((rows, count), F32),
        pltpu.VMEM((rows, count), F32),
        pltpu.VMEM((rows, count), F32),
        pltpu.VMEM((CHUNKS, 2, CHIPS) + right_tile, F32),
        pltpu.VMEM((CHUNKS, 2, CHIPS) + left_tile, F32),
        pltpu.VMEM((CHUNKS, CHIPS) + right_tile, F32),
        pltpu.VMEM((CHUNKS, CHIPS) + left_tile, F32),
        pltpu.VMEM((CHIPS - 1, CHUNKS) + right_tile, F32),
        pltpu.VMEM((CHIPS - 1, CHUNKS) + left_tile, F32),
        pltpu.VMEM((8, count), F32),
        pltpu.VMEM((nz - 1, 8, count), F32),
        dma((CHUNKS,)), dma((CHUNKS,)), dma((CHUNKS,)), dma((CHUNKS,)), dma, dma, dma,
        dma((4,)), dma((4,)), dma((3,)), dma((3,)),
        dma((nz - 1,)), dma((nz - 1,)), dma((CHUNKS, nz - 1)), dma((CHUNKS, nz - 1)),
        dma((nz - 1,)), dma((nz - 1,)),
        dma((2 * CHUNKS,)), dma((2 * CHUNKS,)), dma((2 * CHUNKS, 3)), dma((2 * CHUNKS, 3)),
    ]
    anywhere = pl.BlockSpec(memory_space=pl.ANY)
    vmem = pl.BlockSpec(memory_space=pltpu.VMEM)
    return pl.pallas_call(
        functools.partial(kernel, nz, scale),
        out_shape=(
            jax.ShapeDtypeStruct((blocks_here, rows_left, width), F32),
            jax.ShapeDtypeStruct(right_blocks.shape, F32),
        ),
        in_specs=[anywhere, anywhere, vmem, anywhere, anywhere, anywhere],
        out_specs=(vmem, vmem),
        scratch_shapes=scratch,
        compiler_params=pltpu.CompilerParams(
            collective_id=0, has_side_effects=True, vmem_limit_bytes=60 * 2**20
        ),
        cost_estimate=pl.CostEstimate(flops=5 * 10**9, bytes_accessed=20 * 2**20, transcendentals=0),
    )(alphas, betas, hot, emission, left_blocks, right_blocks)


def local(alphas, betas, token_ids, emission, left_blocks, right_blocks):
    if (
        lax.axis_size("seq") == 2 * CHIPS
        and right_blocks.shape[0] % (8 * CHUNKS) == 0
        and right_blocks.shape[1] % 8 == 0
        and left_blocks.shape[0] % CHUNKS == 0
        and left_blocks.shape[1] % (16 * CHIPS) == 0
    ):
        return fused(alphas, betas, token_ids, emission, left_blocks, right_blocks)
    high = lax.Precision.HIGH
    seq_dev = alphas.shape[1]
    count = 2 * seq_dev
    blocks_here, window, width = left_blocks.shape
    local_k, rows_right, nblocks = right_blocks.shape
    scale = window * nblocks / (2.0 * seq_dev * lax.axis_size("seq"))

    right_full = lax.all_gather(right_blocks, "seq", axis=1, tiled=True)
    a_rows = alphas.reshape(count, blocks_here, width)
    mixed = jnp.einsum("ikj,bij->kib", left_blocks, a_rows, precision=high)
    spread = lax.all_to_all(mixed, "blk", split_axis=0, concat_axis=1, tiled=True)
    rows = jnp.take(emission, token_ids.reshape(count), axis=0)
    signal = (rows * betas.reshape(count, -1)).reshape(count, local_k, nblocks)
    back = jnp.einsum("kim,bkm->kib", right_full, signal, precision=high)
    total = lax.psum(jnp.sum(spread * back, axis=(0, 1)), "blk")
    weight = scale / total
    returned = lax.all_to_all(back, "blk", split_axis=1, concat_axis=0, tiled=True)
    right_sum = jnp.einsum("kib,bkm->ikm", spread * weight, signal, precision=high)
    right_rows = lax.psum_scatter(right_sum, "seq", scatter_dimension=0, tiled=True)
    left_sum = jnp.einsum("kib,bij->kij", returned * weight, a_rows, precision=high)
    left_rows = lax.psum_scatter(left_sum, "seq", scatter_dimension=0, tiled=True)
    return (left_rows.transpose(1, 0, 2), right_rows.transpose(1, 0, 2))


def solution(mesh):
    placed = (
        P(None, "seq", "blk"),
        P(None, "seq", "blk"),
        P(None, "seq"),
        P(None, "blk"),
        P("blk", None, None),
        P("blk", "seq", None),
    )
    return jax.shard_map(
        local,
        mesh=mesh,
        in_specs=placed,
        out_specs=(P("blk", "seq", None), P("blk", "seq", None)),
        check_vma=False,
    )
```

```python
import functools
import jax
import jax.numpy as jnp
from jax import lax
from jax.experimental import pallas as pl
from jax.experimental.pallas import tpu as pltpu
from jax.sharding import PartitionSpec as P

F32 = jnp.float32
BF16 = jnp.bfloat16
CHIPS = 4
CHUNKS = 4


def halves(x):
    top = x.astype(BF16)
    rest = (x - top.astype(F32)).astype(BF16)
    return jnp.concatenate([top, rest], axis=0)


def loop(start, extent, body, unroll):
    def step(n, _):
        for v in range(unroll):
            body(start + n * unroll + v)
        return 0

    lax.fori_loop(0, extent // unroll, step, 0)


def nt(a, b):
    return lax.dot_general(a, b, (((1,), (1,)), ((), ())), preferred_element_type=F32)


def kernel(
    nz, scale, a_hbm, b_hbm, ids_ref, e_hbm, l_hbm, r_hbm, left_own, left_got, right_own, right_got,
    a32, b32, e32, l32, a16, g16, rf, us, ur, hs, hr, pr, pl_, rx0r, rx0l, rxar, rxal, rxbr, rxbl, cs, cr,
    load_a, load_l, load_b, load_e, load_r, own_u, own_h, ag_s, ag_r,
    u_s, u_r, h_s, h_r, c_s, c_r, s0_s, s0_r, s1_s, s1_r, s2_s, s2_r, own_g,
):
    seq = lax.axis_index("seq")
    z = lax.axis_index("blk")
    core, chip = seq % 2, seq // 2
    x, y = chip % 2, chip // 2
    sibling = 2 * chip + 1 - core
    across_x = 2 * (2 * y + 1 - x) + core
    across_y = 2 * (2 * (1 - y) + x) + core
    across = 2 * (2 * (1 - y) + 1 - x) + core
    blocks_here, window, width = l32.shape
    local_k, nblocks = g16.shape[0], g16.shape[2]
    count = a16.shape[1] // 2
    inputs = nz * blocks_here
    tokens = e32.shape[0]
    part_i, part_k = blocks_here // CHUNKS, local_k // CHUNKS
    rows_z = blocks_here * local_k
    rows_c = part_i * local_k

    loads_a, loads_l, loads_b, loads_e = [], [], [], []
    for n in range(CHUNKS):
        cols = pl.ds(n * part_i * width, part_i * width)
        loads_a.append(pltpu.make_async_copy(a_hbm.at[:, :, cols], a32.at[:, :, cols], load_a.at[n]))
        some = pl.ds(n * part_i, part_i)
        loads_l.append(pltpu.make_async_copy(l_hbm.at[some], l32.at[some], load_l.at[n]))
        cols = pl.ds(n * part_k * nblocks, part_k * nblocks)
        loads_b.append(pltpu.make_async_copy(b_hbm.at[:, :, cols], b32.at[:, :, cols], load_b.at[n]))
        loads_e.append(pltpu.make_async_copy(e_hbm.at[:, cols], e32.at[:, cols], load_e.at[n]))
    load_own = pltpu.make_async_copy(r_hbm, rf.at[seq], load_r)
    for n in range(CHUNKS):
        loads_l[n].start()
        loads_a[n].start()
    load_own.start()
    for n in range(CHUNKS):
        loads_e[n].start()
        loads_b[n].start()

    barrier = pltpu.get_barrier_semaphore()
    for other in (sibling, across_x, across_y):
        pl.semaphore_signal(barrier, inc=1, device_id={"seq": other}, device_id_type=pl.DeviceIdType.MESH)
    for d in range(1, nz):
        pl.semaphore_signal(barrier, inc=1, device_id={"blk": (z + d) % nz}, device_id_type=pl.DeviceIdType.MESH)
    pl.semaphore_wait(barrier, 3 + nz - 1)

    def to_seq(src, dst, send, recv, other):
        return pltpu.make_async_remote_copy(
            src_ref=src, dst_ref=dst, send_sem=send, recv_sem=recv,
            device_id={"seq": other}, device_id_type=pl.DeviceIdType.MESH,
        )

    def to_blk(src, dst, send, recv, other):
        return pltpu.make_async_remote_copy(
            src_ref=src, dst_ref=dst, send_sem=send, recv_sem=recv,
            device_id={"blk": other}, device_id_type=pl.DeviceIdType.MESH,
        )

    started = []

    def gather(n, kind, owner, other, lo=0, size=part_k, own=False):
        some = pl.ds(n * part_k + lo, size)
        slot = rf.at[owner, some]
        copy = to_seq(r_hbm.at[some] if own else slot, slot, ag_s.at[kind, n], ag_r.at[kind, n], other)
        copy.start()
        started.append(copy)
        return copy

    gx, gy, gs, gd, fx, fy, fd = {}, {}, {}, {}, {}, {}, {}
    for n in range(CHUNKS):
        gx[n] = gather(n, 0, seq, across_x, own=True)
        gy[n] = gather(n, 1, seq, across_y, own=True)
        gs[n] = gather(n, 2, seq, sibling, own=True)

    def near(n):
        half = part_k // 2
        gx[n].wait_recv()
        relay_y = gather(n, 3, across_x, across_y, 0, half)
        fx[n] = gather(n, 5, across_x, sibling)
        gy[n].wait_recv()
        relay_x = gather(n, 4, across_y, across_x, half, half)
        fy[n] = gather(n, 6, across_y, sibling)
        gd[n] = (relay_y, relay_x)

    def far(n):
        for copy in gd[n]:
            copy.wait_recv()
        fd[n] = gather(n, 7, across, sibling)

    def u_block(i):
        cols = pl.ds(pl.multiple_of(i * width, width), width)
        a = halves(jnp.concatenate([a32[0, :, cols], a32[1, :, cols]], axis=0))
        a16[i] = a
        both = nt(halves(l32[i]), a)
        u = both[:window, :count] + both[:window, count:] + both[window:, :count]
        for dz in range(nz):
            us[pl.ds(dz * rows_z + i * local_k, local_k), :] = u[dz * local_k:(dz + 1) * local_k]

    u_sends = []
    for n in range(CHUNKS):
        loads_l[n].wait()
        loads_a[n].wait()
        loop(n * part_i, part_i, u_block, 2)
        for d in range(1, nz):
            other = (z + d) % nz
            copy = to_blk(
                us.at[pl.ds(other * rows_z + n * rows_c, rows_c)],
                ur.at[pl.ds(z * rows_z + n * rows_c, rows_c)],
                u_s.at[n, d - 1], u_r.at[n, d - 1], other,
            )
            copy.start()
            u_sends.append(copy)
    u_own = pltpu.make_async_copy(us.at[pl.ds(z * rows_z, rows_z)], ur.at[pl.ds(z * rows_z, rows_z)], own_u)
    u_own.start()

    token = lax.broadcasted_iota(jnp.int32, (128, count // 2), 0) % tokens
    hot = jnp.concatenate(
        [jnp.where(token == ids_ref[t:t + 1, :], 1.0, 0.0).astype(F32) for t in range(2)], axis=1
    )
    hot = jnp.transpose(hot)[:, :3 * tokens].astype(BF16)

    def g_block(k):
        cols = pl.ds(pl.multiple_of(k * nblocks, nblocks), nblocks)
        e = e32[:, cols]
        e1 = e.astype(BF16)
        rest = e - e1.astype(F32)
        e2 = rest.astype(BF16)
        e3 = (rest - e2.astype(F32)).astype(BF16)
        picked = jnp.dot(hot, jnp.concatenate([e1, e2, e3], axis=0), preferred_element_type=F32)
        b = jnp.concatenate([b32[0, :, cols], b32[1, :, cols]], axis=0)
        g16[k] = halves(picked * b)

    def h_block(k):
        r = halves(jnp.concatenate([rf[s, k] for s in range(2 * CHIPS)], axis=0))
        both = nt(r, g16[k])
        h = both[:inputs, :count] + both[:inputs, count:] + both[inputs:, :count]
        hs[pl.ds(k, inputs, stride=local_k), :] = h

    def h_part(n):
        if n == 0:
            load_own.wait()
        for copies in (gs, fx, fy, fd):
            copies[n].wait_recv()
        loop(n * part_k, part_k, h_block, 4)

    for n in range(CHUNKS):
        loads_e[n].wait()
        loads_b[n].wait()
        loop(n * part_k, part_k, g_block, 4)
        near(n)
        if n >= 1:
            far(n - 1)
        if n >= 2:
            h_part(n - 2)
    far(CHUNKS - 1)
    h_part(CHUNKS - 2)
    h_part(CHUNKS - 1)

    u_own.wait()
    for copy in u_sends:
        copy.wait_recv()
    step = 64

    def c_block(n, acc):
        rows = pl.ds(pl.multiple_of(n * step, step), step)
        return acc + jnp.sum((ur[rows, :] * hs[rows, :]).reshape(step // 8, 8, count), axis=0)

    acc = lax.fori_loop(0, nz * rows_z // step, c_block, jnp.zeros((8, count), F32))
    cs[...] = acc
    c_sends = []
    for d in range(1, nz):
        copy = to_blk(cs, cr.at[d - 1], c_s.at[d - 1], c_r.at[d - 1], (z + d) % nz)
        copy.start()
        c_sends.append(copy)
    h_own = pltpu.make_async_copy(hs.at[pl.ds(z * rows_z, rows_z)], hr.at[pl.ds(z * rows_z, rows_z)], own_h)
    h_own.start()
    h_sends = []
    for n in range(CHUNKS):
        for d in range(1, nz):
            other = (z + d) % nz
            copy = to_blk(
                hs.at[pl.ds(other * rows_z + n * rows_c, rows_c)],
                hr.at[pl.ds(z * rows_z + n * rows_c, rows_c)],
                h_s.at[n, d - 1], h_r.at[n, d - 1], other,
            )
            copy.start()
            h_sends.append(copy)
    total = acc
    for n, copy in enumerate(c_sends):
        copy.wait_recv()
        total = total + cr[n]
    weight = scale / jnp.sum(total, axis=0, keepdims=True)

    def right_part(n):
        def block(kk):
            k = n * part_k + kk
            u = halves(ur[pl.ds(k, inputs, stride=local_k), :] * weight)
            both = jnp.dot(jnp.concatenate([u, u], axis=1), g16[k], preferred_element_type=F32)
            grad = both[:inputs] + both[inputs:]
            rows = inputs // (2 * CHIPS)
            for s in range(2 * CHIPS):
                pr[n, s % 2, s // 4, s // 2 % 2, kk] = grad[s * rows:(s + 1) * rows]

        loop(0, part_k, block, 4)

    def left_part(n):
        def block(ii):
            i = n * part_i + ii
            h = jnp.concatenate(
                [hr[pl.ds(pl.multiple_of(sz * rows_z + i * local_k, local_k), local_k), :] for sz in range(nz)], axis=0
            )
            h = halves(h * weight)
            both = jnp.dot(jnp.concatenate([h, h], axis=1), a16[i], preferred_element_type=F32)
            grad = both[:window] + both[window:]
            rows = window // (2 * CHIPS)
            for s in range(2 * CHIPS):
                pl_[n, s % 2, s // 4, s // 2 % 2, ii] = grad[s * rows:(s + 1) * rows]

        loop(0, part_i, block, 2)

    firsts, seconds, thirds, kept = {}, {}, {}, []

    def first(m):
        mine, rx0 = (pr, rx0r) if m < CHUNKS else (pl_, rx0l)
        n = m % CHUNKS
        firsts[m] = to_seq(mine.at[n, 1 - core], rx0.at[n], s0_s.at[m], s0_r.at[m], sibling)
        firsts[m].start()

    def second(m):
        mine, rx0, rxa, rxb = (pr, rx0r, rxar, rxbr) if m < CHUNKS else (pl_, rx0l, rxal, rxbl)
        n = m % CHUNKS
        half = mine.shape[4] // 2
        firsts[m].wait_recv()
        for p in range(2):
            for q in range(2):
                mine[n, core, p, q] = mine[n, core, p, q] + rx0[n, p, q]
        copy_x = to_seq(
            mine.at[n, core, :, 1 - x, pl.ds(0, half)], rxa.at[n], s1_s.at[m, 0], s1_r.at[m, 0], across_x
        )
        copy_y = to_seq(
            mine.at[n, core, 1 - y, :, pl.ds(half, half)], rxb.at[n], s1_s.at[m, 1], s1_r.at[m, 1], across_y
        )
        copy_x.start()
        copy_y.start()
        seconds[m] = (copy_x, copy_y)

    def third(m):
        mine, rxa, rxb, own, got = (
            (pr, rxar, rxbr, right_own, right_got) if m < CHUNKS else (pl_, rxal, rxbl, left_own, left_got)
        )
        n = m % CHUNKS
        part = mine.shape[4]
        half = part // 2
        low, top = pl.ds(0, half), pl.ds(half, half)
        seconds[m][0].wait_recv()
        mine[n, core, 1 - y, x, low] = mine[n, core, 1 - y, x, low] + rxa[n, 1 - y]
        copy_y = to_seq(
            mine.at[n, core, 1 - y, x, low], got.at[pl.ds(n * part, half)], s2_s.at[m, 0], s2_r.at[m, 0], across_y
        )
        copy_y.start()
        seconds[m][1].wait_recv()
        mine[n, core, y, 1 - x, top] = mine[n, core, y, 1 - x, top] + rxb[n, 1 - x]
        copy_x = to_seq(
            mine.at[n, core, y, 1 - x, top], got.at[pl.ds(n * part + half, half)], s2_s.at[m, 1], s2_r.at[m, 1], across_x
        )
        copy_x.start()
        thirds[m] = (copy_y, copy_x)
        mine[n, core, y, x, low] = mine[n, core, y, x, low] + rxa[n, y]
        mine[n, core, y, x, top] = mine[n, core, y, x, top] + rxb[n, x]
        keep = pltpu.make_async_copy(mine.at[n, core, y, x], own.at[pl.ds(n * part, part)], own_g.at[m])
        keep.start()
        kept.append(keep)

    for m in range(2 * CHUNKS):
        n = m % CHUNKS
        if m < CHUNKS:
            right_part(n)
        else:
            if n == 0:
                h_own.wait()
            for copy in h_sends[n * (nz - 1):(n + 1) * (nz - 1)]:
                copy.wait_recv()
            left_part(n)
        first(m)
        if m >= 1:
            second(m - 1)
        if m >= 2:
            third(m - 2)
    second(2 * CHUNKS - 1)
    third(2 * CHUNKS - 2)
    third(2 * CHUNKS - 1)

    for copies in thirds.values():
        for copy in copies:
            copy.wait()
    for copy in kept:
        copy.wait()
    for copy in started + u_sends + c_sends + h_sends + list(firsts.values()):
        copy.wait_send()
    for copies in seconds.values():
        for copy in copies:
            copy.wait_send()


def fused(alphas, betas, token_ids, emission, left_blocks, right_blocks):
    nz = lax.axis_size("blk")
    seq_dev = alphas.shape[1]
    count = 2 * seq_dev
    blocks_here, window, width = left_blocks.shape
    local_k, rows_right, nblocks = right_blocks.shape
    rows_left = window // (2 * CHIPS)
    scale = window * nblocks / (2.0 * seq_dev * lax.axis_size("seq"))
    part_i, part_k = blocks_here // CHUNKS, local_k // CHUNKS
    rows = nz * blocks_here * local_k
    dma = pltpu.SemaphoreType.DMA
    left_tile = (part_i, rows_left, width)
    right_tile = (part_k, rows_right, nblocks)
    left_half = (part_i // 2, rows_left, width)
    right_half = (part_k // 2, rows_right, nblocks)
    scratch = [
        pltpu.VMEM(alphas.shape, F32),
        pltpu.VMEM(betas.shape, F32),
        pltpu.VMEM(emission.shape, F32),
        pltpu.VMEM(left_blocks.shape, F32),
        pltpu.VMEM((blocks_here, 2 * count, width), BF16),
        pltpu.VMEM((local_k, 2 * count, nblocks), BF16),
        pltpu.VMEM((2 * CHIPS,) + right_blocks.shape, F32),
        pltpu.VMEM((rows, count), F32),
        pltpu.VMEM((rows, count), F32),
        pltpu.VMEM((rows, count), F32),
        pltpu.VMEM((rows, count), F32),
        pltpu.VMEM((CHUNKS, 2, 2, 2) + right_tile, F32),
        pltpu.VMEM((CHUNKS, 2, 2, 2) + left_tile, F32),
        pltpu.VMEM((CHUNKS, 2, 2) + right_tile, F32),
        pltpu.VMEM((CHUNKS, 2, 2) + left_tile, F32),
        pltpu.VMEM((CHUNKS, 2) + right_half, F32),
        pltpu.VMEM((CHUNKS, 2) + left_half, F32),
        pltpu.VMEM((CHUNKS, 2) + right_half, F32),
        pltpu.VMEM((CHUNKS, 2) + left_half, F32),
        pltpu.VMEM((8, count), F32),
        pltpu.VMEM((nz - 1, 8, count), F32),
        dma((CHUNKS,)), dma((CHUNKS,)), dma((CHUNKS,)), dma((CHUNKS,)), dma, dma, dma,
        dma((8, CHUNKS)), dma((8, CHUNKS)),
        dma((CHUNKS, nz - 1)), dma((CHUNKS, nz - 1)), dma((CHUNKS, nz - 1)), dma((CHUNKS, nz - 1)),
        dma((nz - 1,)), dma((nz - 1,)),
        dma((2 * CHUNKS,)), dma((2 * CHUNKS,)), dma((2 * CHUNKS, 2)), dma((2 * CHUNKS, 2)),
        dma((2 * CHUNKS, 2)), dma((2 * CHUNKS, 2)), dma((2 * CHUNKS,)),
    ]
    anywhere = pl.BlockSpec(memory_space=pl.ANY)
    vmem = pl.BlockSpec(memory_space=pltpu.VMEM)
    left_out = jax.ShapeDtypeStruct((blocks_here, rows_left, width), F32)
    right_out = jax.ShapeDtypeStruct(right_blocks.shape, F32)
    left_own, left_got, right_own, right_got = pl.pallas_call(
        functools.partial(kernel, nz, scale),
        out_shape=(left_out, left_out, right_out, right_out),
        in_specs=[anywhere, anywhere, vmem, anywhere, anywhere, anywhere],
        out_specs=(anywhere,) * 4,
        scratch_shapes=scratch,
        compiler_params=pltpu.CompilerParams(
            collective_id=0, has_side_effects=True, vmem_limit_bytes=60 * 2**20
        ),
        cost_estimate=pl.CostEstimate(flops=5 * 10**9, bytes_accessed=20 * 2**20, transcendentals=0),
    )(alphas, betas, token_ids, emission, left_blocks, right_blocks)
    return (left_own + left_got, right_own + right_got)


def local(alphas, betas, token_ids, emission, left_blocks, right_blocks):
    if (
        lax.axis_size("seq") == 2 * CHIPS
        and right_blocks.shape[0] % (8 * CHUNKS) == 0
        and right_blocks.shape[1] % 8 == 0
        and left_blocks.shape[0] % (2 * CHUNKS) == 0
        and 3 * emission.shape[0] <= 128
        and left_blocks.shape[1] % (16 * CHIPS) == 0
    ):
        return fused(alphas, betas, token_ids, emission, left_blocks, right_blocks)
    high = lax.Precision.HIGH
    seq_dev = alphas.shape[1]
    count = 2 * seq_dev
    blocks_here, window, width = left_blocks.shape
    local_k, rows_right, nblocks = right_blocks.shape
    scale = window * nblocks / (2.0 * seq_dev * lax.axis_size("seq"))

    right_full = lax.all_gather(right_blocks, "seq", axis=1, tiled=True)
    a_rows = alphas.reshape(count, blocks_here, width)
    mixed = jnp.einsum("ikj,bij->kib", left_blocks, a_rows, precision=high)
    spread = lax.all_to_all(mixed, "blk", split_axis=0, concat_axis=1, tiled=True)
    rows = jnp.take(emission, token_ids.reshape(count), axis=0)
    signal = (rows * betas.reshape(count, -1)).reshape(count, local_k, nblocks)
    back = jnp.einsum("kim,bkm->kib", right_full, signal, precision=high)
    total = lax.psum(jnp.sum(spread * back, axis=(0, 1)), "blk")
    weight = scale / total
    returned = lax.all_to_all(back, "blk", split_axis=1, concat_axis=0, tiled=True)
    right_sum = jnp.einsum("kib,bkm->ikm", spread * weight, signal, precision=high)
    right_rows = lax.psum_scatter(right_sum, "seq", scatter_dimension=0, tiled=True)
    left_sum = jnp.einsum("kib,bij->kij", returned * weight, a_rows, precision=high)
    left_rows = lax.psum_scatter(left_sum, "seq", scatter_dimension=0, tiled=True)
    return (left_rows.transpose(1, 0, 2), right_rows.transpose(1, 0, 2))


def solution(mesh):
    placed = (
        P(None, "seq", "blk"),
        P(None, "seq", "blk"),
        P(None, "seq"),
        P(None, "blk"),
        P("blk", None, None),
        P("blk", "seq", None),
    )
    return jax.shard_map(
        local,
        mesh=mesh,
        in_specs=placed,
        out_specs=(P("blk", "seq", None), P("blk", "seq", None)),
        check_vma=False,
    )
```

```python
import functools
import jax
import jax.numpy as jnp
from jax import lax
from jax.experimental import pallas as pl
from jax.experimental.pallas import tpu as pltpu
from jax.sharding import PartitionSpec as P

F32 = jnp.float32
BF16 = jnp.bfloat16
CHIPS = 4
PARTS = 4
CHUNKS = 8


def halves(x):
    top = x.astype(BF16)
    rest = (x - top.astype(F32)).astype(BF16)
    return jnp.concatenate([top, rest], axis=0)


def loop(start, extent, body, unroll):
    def step(n, _):
        for v in range(unroll):
            body(start + n * unroll + v)
        return 0

    lax.fori_loop(0, extent // unroll, step, 0)


def nt(a, b):
    return lax.dot_general(a, b, (((1,), (1,)), ((), ())), preferred_element_type=F32)


def kernel(
    nz, scale, a_hbm, b_hbm, ids_ref, e_hbm, l_hbm, r_hbm, left_own, left_got, right_own, right_got,
    a32, b32, e32, l32, a16, g16, rf, us, ur, hs, hr, pr, pl_, rx0r, rx0l, rxar, rxal, rxbr, rxbl, cs, cr,
    load_a, load_l, load_b, load_e, load_r, own_u, own_h, ag_s, ag_r,
    u_s, u_r, h_s, h_r, c_s, c_r, s0_s, s0_r, s1_s, s1_r, s2_s, s2_r, own_g,
):
    seq = lax.axis_index("seq")
    z = lax.axis_index("blk")
    core, chip = seq % 2, seq // 2
    x, y = chip % 2, chip // 2
    sibling = 2 * chip + 1 - core
    across_x = 2 * (2 * y + 1 - x) + core
    across_y = 2 * (2 * (1 - y) + x) + core
    across = 2 * (2 * (1 - y) + 1 - x) + core
    blocks_here, window, width = l32.shape
    local_k, nblocks = g16.shape[0], g16.shape[2]
    count = a16.shape[1] // 2
    inputs = nz * blocks_here
    tokens = e32.shape[0]
    part_i, part_k = blocks_here // PARTS, local_k // PARTS
    rows_z = blocks_here * local_k
    rows_c = part_i * local_k

    loads_a, loads_l, loads_b, loads_e = [], [], [], []
    for n in range(PARTS):
        cols = pl.ds(n * part_i * width, part_i * width)
        loads_a.append(pltpu.make_async_copy(a_hbm.at[:, :, cols], a32.at[:, :, cols], load_a.at[n]))
        some = pl.ds(n * part_i, part_i)
        loads_l.append(pltpu.make_async_copy(l_hbm.at[some], l32.at[some], load_l.at[n]))
        cols = pl.ds(n * part_k * nblocks, part_k * nblocks)
        loads_b.append(pltpu.make_async_copy(b_hbm.at[:, :, cols], b32.at[:, :, cols], load_b.at[n]))
        loads_e.append(pltpu.make_async_copy(e_hbm.at[:, cols], e32.at[:, cols], load_e.at[n]))
    load_own = pltpu.make_async_copy(r_hbm, rf.at[seq], load_r)
    for n in range(PARTS):
        loads_l[n].start()
        loads_a[n].start()
    load_own.start()

    steps = (2, 3 - 2 * (z % 2), 1 + 2 * (z % 2)) if nz == 4 else tuple(range(1, nz))

    barrier = pltpu.get_barrier_semaphore()
    for other in (sibling, across_x, across_y):
        pl.semaphore_signal(barrier, inc=1, device_id={"seq": other}, device_id_type=pl.DeviceIdType.MESH)
    for d in range(1, nz):
        pl.semaphore_signal(barrier, inc=1, device_id={"blk": (z + d) % nz}, device_id_type=pl.DeviceIdType.MESH)

    def to_seq(src, dst, send, recv, other):
        return pltpu.make_async_remote_copy(
            src_ref=src, dst_ref=dst, send_sem=send, recv_sem=recv,
            device_id={"seq": other}, device_id_type=pl.DeviceIdType.MESH,
        )

    def to_blk(src, dst, send, recv, other):
        return pltpu.make_async_remote_copy(
            src_ref=src, dst_ref=dst, send_sem=send, recv_sem=recv,
            device_id={"blk": other}, device_id_type=pl.DeviceIdType.MESH,
        )

    started = []

    def gather(n, kind, owner, other, lo=0, size=local_k // PARTS, own=False):
        some = pl.ds(n * (local_k // PARTS) + lo, size)
        slot = rf.at[owner, some]
        copy = to_seq(r_hbm.at[some] if own else slot, slot, ag_s.at[kind, n], ag_r.at[kind, n], other)
        copy.start()
        started.append(copy)
        return copy

    gx, gy, gs, gd, fx, fy, fd = {}, {}, {}, {}, {}, {}, {}

    def near(n):
        half = part_k // 2
        gx[n].wait_recv()
        relay_y = gather(n, 3, across_x, across_y, 0, half)
        fx[n] = gather(n, 5, across_x, sibling)
        gy[n].wait_recv()
        relay_x = gather(n, 4, across_y, across_x, half, half)
        fy[n] = gather(n, 6, across_y, sibling)
        gd[n] = (relay_y, relay_x)

    def far(n):
        for copy in gd[n]:
            copy.wait_recv()
        fd[n] = gather(n, 7, across, sibling)

    def u_block(i):
        cols = pl.ds(pl.multiple_of(i * width, width), width)
        a = halves(jnp.concatenate([a32[0, :, cols], a32[1, :, cols]], axis=0))
        a16[i] = a
        both = nt(halves(l32[i]), a)
        u = both[:window, :count] + both[:window, count:] + both[window:, :count]
        for dz in range(nz):
            us[pl.ds(dz * rows_z + i * local_k, local_k), :] = u[dz * local_k:(dz + 1) * local_k]

    u_sends = []
    for n in range(PARTS):
        loads_l[n].wait()
        loads_a[n].wait()
        loop(n * part_i, part_i, u_block, 2)
        if n == 0:
            pl.semaphore_wait(barrier, 3 + nz - 1)
        for o, d in enumerate(steps):
            other = (z + d) % nz
            copy = to_blk(
                us.at[pl.ds(other * rows_z + n * rows_c, rows_c)],
                ur.at[pl.ds(z * rows_z + n * rows_c, rows_c)],
                u_s.at[n, o], u_r.at[n, o], other,
            )
            copy.start()
            u_sends.append(copy)
        if n == 0:
            for p in range(PARTS):
                gx[p] = gather(p, 0, seq, across_x, own=True)
                gy[p] = gather(p, 1, seq, across_y, own=True)
                gs[p] = gather(p, 2, seq, sibling, own=True)
        loads_e[n].start()
        loads_b[n].start()
    u_own = pltpu.make_async_copy(us.at[pl.ds(z * rows_z, rows_z)], ur.at[pl.ds(z * rows_z, rows_z)], own_u)
    u_own.start()

    token = lax.broadcasted_iota(jnp.int32, (128, count // 2), 0) % tokens
    hot = jnp.concatenate(
        [jnp.where(token == ids_ref[t:t + 1, :], 1.0, 0.0).astype(F32) for t in range(2)], axis=1
    )
    hot = jnp.transpose(hot)[:, :3 * tokens].astype(BF16)

    def g_block(k):
        cols = pl.ds(pl.multiple_of(k * nblocks, nblocks), nblocks)
        e = e32[:, cols]
        e1 = e.astype(BF16)
        rest = e - e1.astype(F32)
        e2 = rest.astype(BF16)
        e3 = (rest - e2.astype(F32)).astype(BF16)
        picked = jnp.dot(hot, jnp.concatenate([e1, e2, e3], axis=0), preferred_element_type=F32)
        b = jnp.concatenate([b32[0, :, cols], b32[1, :, cols]], axis=0)
        g16[k] = halves(picked * b)

    def h_block(k):
        r = halves(jnp.concatenate([rf[s, k] for s in range(2 * CHIPS)], axis=0))
        both = nt(r, g16[k])
        h = both[:inputs, :count] + both[:inputs, count:] + both[inputs:, :count]
        hs[pl.ds(k, inputs, stride=local_k), :] = h

    def h_part(n):
        if n == 0:
            load_own.wait()
        for copies in (gs, fx, fy, fd):
            copies[n].wait_recv()
        loop(n * part_k, part_k, h_block, 4)

    for n in range(PARTS):
        loads_e[n].wait()
        loads_b[n].wait()
        loop(n * part_k, part_k, g_block, 4)
        near(n)
        if n >= 1:
            far(n - 1)
        if n >= 2:
            h_part(n - 2)
    far(PARTS - 1)
    h_part(PARTS - 2)
    h_part(PARTS - 1)

    step = 64
    acc = jnp.zeros((8, count), F32)
    u_own.wait()
    for n in range(PARTS):
        for copy in u_sends[n * (nz - 1):(n + 1) * (nz - 1)]:
            copy.wait_recv()
        for sz in range(nz):
            for lo in range(0, rows_c, step):
                rows = pl.ds(sz * rows_z + n * rows_c + lo, step)
                acc = acc + jnp.sum((ur[rows, :] * hs[rows, :]).reshape(step // 8, 8, count), axis=0)
    cs[...] = acc
    c_sends = []
    for d in range(1, nz):
        copy = to_blk(cs, cr.at[d - 1], c_s.at[d - 1], c_r.at[d - 1], (z + d) % nz)
        copy.start()
        c_sends.append(copy)
    h_own = pltpu.make_async_copy(hs.at[pl.ds(z * rows_z, rows_z)], hr.at[pl.ds(z * rows_z, rows_z)], own_h)
    h_own.start()
    part_i, part_k = blocks_here // CHUNKS, local_k // CHUNKS
    rows_c = part_i * local_k
    h_sends = []
    for n in range(CHUNKS):
        for o, d in enumerate(steps):
            other = (z + d) % nz
            copy = to_blk(
                hs.at[pl.ds(other * rows_z + n * rows_c, rows_c)],
                hr.at[pl.ds(z * rows_z + n * rows_c, rows_c)],
                h_s.at[n, o], h_r.at[n, o], other,
            )
            copy.start()
            h_sends.append(copy)
    total = acc
    for n, copy in enumerate(c_sends):
        copy.wait_recv()
        total = total + cr[n]
    weight = scale / jnp.sum(total, axis=0, keepdims=True)

    def right_part(n):
        def block(kk):
            k = n * part_k + kk
            u = halves(ur[pl.ds(k, inputs, stride=local_k), :] * weight)
            both = jnp.dot(jnp.concatenate([u, u], axis=1), g16[k], preferred_element_type=F32)
            grad = both[:inputs] + both[inputs:]
            rows = inputs // (2 * CHIPS)
            for s in range(2 * CHIPS):
                pr[n, s % 2, s // 4, s // 2 % 2, kk] = grad[s * rows:(s + 1) * rows]

        loop(0, part_k, block, 4)

    def left_part(n):
        def block(ii):
            i = n * part_i + ii
            h = jnp.concatenate(
                [hr[pl.ds(pl.multiple_of(sz * rows_z + i * local_k, local_k), local_k), :] for sz in range(nz)], axis=0
            )
            h = halves(h * weight)
            both = jnp.dot(jnp.concatenate([h, h], axis=1), a16[i], preferred_element_type=F32)
            grad = both[:window] + both[window:]
            rows = window // (2 * CHIPS)
            for s in range(2 * CHIPS):
                pl_[n, s % 2, s // 4, s // 2 % 2, ii] = grad[s * rows:(s + 1) * rows]

        loop(0, part_i, block, 2)

    firsts, seconds, thirds, kept = {}, {}, {}, []

    def first(m):
        mine, rx0 = (pr, rx0r) if m < CHUNKS else (pl_, rx0l)
        n = m % CHUNKS
        firsts[m] = to_seq(mine.at[n, 1 - core], rx0.at[n], s0_s.at[m], s0_r.at[m], sibling)
        firsts[m].start()

    def second(m):
        mine, rx0, rxa, rxb = (pr, rx0r, rxar, rxbr) if m < CHUNKS else (pl_, rx0l, rxal, rxbl)
        n = m % CHUNKS
        half = mine.shape[4] // 2
        firsts[m].wait_recv()
        for p in range(2):
            for q in range(2):
                mine[n, core, p, q] = mine[n, core, p, q] + rx0[n, p, q]
        copy_x = to_seq(
            mine.at[n, core, :, 1 - x, pl.ds(0, half)], rxa.at[n], s1_s.at[m, 0], s1_r.at[m, 0], across_x
        )
        copy_y = to_seq(
            mine.at[n, core, 1 - y, :, pl.ds(half, half)], rxb.at[n], s1_s.at[m, 1], s1_r.at[m, 1], across_y
        )
        copy_x.start()
        copy_y.start()
        seconds[m] = (copy_x, copy_y)

    def third(m):
        mine, rxa, rxb, own, got = (
            (pr, rxar, rxbr, right_own, right_got) if m < CHUNKS else (pl_, rxal, rxbl, left_own, left_got)
        )
        n = m % CHUNKS
        part = mine.shape[4]
        half = part // 2
        low, top = pl.ds(0, half), pl.ds(half, half)
        seconds[m][0].wait_recv()
        mine[n, core, 1 - y, x, low] = mine[n, core, 1 - y, x, low] + rxa[n, 1 - y]
        copy_y = to_seq(
            mine.at[n, core, 1 - y, x, low], got.at[pl.ds(n * part, half)], s2_s.at[m, 0], s2_r.at[m, 0], across_y
        )
        copy_y.start()
        seconds[m][1].wait_recv()
        mine[n, core, y, 1 - x, top] = mine[n, core, y, 1 - x, top] + rxb[n, 1 - x]
        copy_x = to_seq(
            mine.at[n, core, y, 1 - x, top], got.at[pl.ds(n * part + half, half)], s2_s.at[m, 1], s2_r.at[m, 1], across_x
        )
        copy_x.start()
        thirds[m] = (copy_y, copy_x)
        mine[n, core, y, x, low] = mine[n, core, y, x, low] + rxa[n, y]
        mine[n, core, y, x, top] = mine[n, core, y, x, top] + rxb[n, x]
        keep = pltpu.make_async_copy(mine.at[n, core, y, x], own.at[pl.ds(n * part, part)], own_g.at[m])
        keep.start()
        kept.append(keep)

    for m in range(2 * CHUNKS):
        n = m % CHUNKS
        if m < CHUNKS:
            right_part(n)
            first(m)
        if m >= 1:
            second(m - 1)
        if m >= 2:
            third(m - 2)
        if m >= CHUNKS:
            if n == 0:
                h_own.wait()
            for copy in h_sends[n * (nz - 1):(n + 1) * (nz - 1)]:
                copy.wait_recv()
            left_part(n)
            first(m)
    second(2 * CHUNKS - 1)
    third(2 * CHUNKS - 2)
    third(2 * CHUNKS - 1)

    for copies in thirds.values():
        for copy in copies:
            copy.wait()
    for copy in kept:
        copy.wait()
    for copy in started + u_sends + c_sends + h_sends + list(firsts.values()):
        copy.wait_send()
    for copies in seconds.values():
        for copy in copies:
            copy.wait_send()


def last_sum(left_own, left_got, right_own, right_got, left, right):
    left[...] = left_own[...] + left_got[...]
    right[...] = right_own[...] + right_got[...]


def fused(alphas, betas, token_ids, emission, left_blocks, right_blocks):
    nz = lax.axis_size("blk")
    seq_dev = alphas.shape[1]
    count = 2 * seq_dev
    blocks_here, window, width = left_blocks.shape
    local_k, rows_right, nblocks = right_blocks.shape
    rows_left = window // (2 * CHIPS)
    scale = window * nblocks / (2.0 * seq_dev * lax.axis_size("seq"))
    part_i, part_k = blocks_here // CHUNKS, local_k // CHUNKS
    rows = nz * blocks_here * local_k
    dma = pltpu.SemaphoreType.DMA
    left_tile = (part_i, rows_left, width)
    right_tile = (part_k, rows_right, nblocks)
    left_half = (part_i // 2, rows_left, width)
    right_half = (part_k // 2, rows_right, nblocks)
    scratch = [
        pltpu.VMEM(alphas.shape, F32),
        pltpu.VMEM(betas.shape, F32),
        pltpu.VMEM(emission.shape, F32),
        pltpu.VMEM(left_blocks.shape, F32),
        pltpu.VMEM((blocks_here, 2 * count, width), BF16),
        pltpu.VMEM((local_k, 2 * count, nblocks), BF16),
        pltpu.VMEM((2 * CHIPS,) + right_blocks.shape, F32),
        pltpu.VMEM((rows, count), F32),
        pltpu.VMEM((rows, count), F32),
        pltpu.VMEM((rows, count), F32),
        pltpu.VMEM((rows, count), F32),
        pltpu.VMEM((CHUNKS, 2, 2, 2) + right_tile, F32),
        pltpu.VMEM((CHUNKS, 2, 2, 2) + left_tile, F32),
        pltpu.VMEM((CHUNKS, 2, 2) + right_tile, F32),
        pltpu.VMEM((CHUNKS, 2, 2) + left_tile, F32),
        pltpu.VMEM((CHUNKS, 2) + right_half, F32),
        pltpu.VMEM((CHUNKS, 2) + left_half, F32),
        pltpu.VMEM((CHUNKS, 2) + right_half, F32),
        pltpu.VMEM((CHUNKS, 2) + left_half, F32),
        pltpu.VMEM((8, count), F32),
        pltpu.VMEM((nz - 1, 8, count), F32),
        dma((PARTS,)), dma((PARTS,)), dma((PARTS,)), dma((PARTS,)), dma, dma, dma,
        dma((8, PARTS)), dma((8, PARTS)),
        dma((PARTS, nz - 1)), dma((PARTS, nz - 1)), dma((CHUNKS, nz - 1)), dma((CHUNKS, nz - 1)),
        dma((nz - 1,)), dma((nz - 1,)),
        dma((2 * CHUNKS,)), dma((2 * CHUNKS,)), dma((2 * CHUNKS, 2)), dma((2 * CHUNKS, 2)),
        dma((2 * CHUNKS, 2)), dma((2 * CHUNKS, 2)), dma((2 * CHUNKS,)),
    ]
    anywhere = pl.BlockSpec(memory_space=pl.ANY)
    vmem = pl.BlockSpec(memory_space=pltpu.VMEM)
    left_out = jax.ShapeDtypeStruct((blocks_here, rows_left, width), F32)
    right_out = jax.ShapeDtypeStruct(right_blocks.shape, F32)
    left_own, left_got, right_own, right_got = pl.pallas_call(
        functools.partial(kernel, nz, scale),
        out_shape=(left_out, left_out, right_out, right_out),
        in_specs=[anywhere, anywhere, vmem, anywhere, anywhere, anywhere],
        out_specs=(anywhere,) * 4,
        scratch_shapes=scratch,
        compiler_params=pltpu.CompilerParams(
            collective_id=0, has_side_effects=True, vmem_limit_bytes=60 * 2**20
        ),
        cost_estimate=pl.CostEstimate(flops=5 * 10**9, bytes_accessed=20 * 2**20, transcendentals=0),
    )(alphas, betas, token_ids, emission, left_blocks, right_blocks)
    flat = (-1, width)
    grid = 4
    left, right = pl.pallas_call(
        last_sum,
        grid=(grid,),
        out_shape=(
            jax.ShapeDtypeStruct((left_own.size // width, width), F32),
            jax.ShapeDtypeStruct((right_own.size // width, width), F32),
        ),
        in_specs=[
            pl.BlockSpec((part.size // width // grid, width), lambda n: (n, 0))
            for part in (left_own, left_got, right_own, right_got)
        ],
        out_specs=tuple(
            pl.BlockSpec((part.size // width // grid, width), lambda n: (n, 0)) for part in (left_own, right_own)
        ),
        compiler_params=pltpu.CompilerParams(vmem_limit_bytes=60 * 2**20),
    )(left_own.reshape(flat), left_got.reshape(flat), right_own.reshape(flat), right_got.reshape(flat))
    return left.reshape(left_own.shape), right.reshape(right_own.shape)


def local(alphas, betas, token_ids, emission, left_blocks, right_blocks):
    if (
        lax.axis_size("seq") == 2 * CHIPS
        and right_blocks.shape[0] % (4 * CHUNKS) == 0
        and right_blocks.shape[2] == left_blocks.shape[2]
        and right_blocks.shape[1] % 8 == 0
        and left_blocks.shape[0] % (2 * CHUNKS) == 0
        and 3 * emission.shape[0] <= 128
        and left_blocks.shape[1] % (16 * CHIPS) == 0
    ):
        return fused(alphas, betas, token_ids, emission, left_blocks, right_blocks)
    high = lax.Precision.HIGH
    seq_dev = alphas.shape[1]
    count = 2 * seq_dev
    blocks_here, window, width = left_blocks.shape
    local_k, rows_right, nblocks = right_blocks.shape
    scale = window * nblocks / (2.0 * seq_dev * lax.axis_size("seq"))

    right_full = lax.all_gather(right_blocks, "seq", axis=1, tiled=True)
    a_rows = alphas.reshape(count, blocks_here, width)
    mixed = jnp.einsum("ikj,bij->kib", left_blocks, a_rows, precision=high)
    spread = lax.all_to_all(mixed, "blk", split_axis=0, concat_axis=1, tiled=True)
    rows = jnp.take(emission, token_ids.reshape(count), axis=0)
    signal = (rows * betas.reshape(count, -1)).reshape(count, local_k, nblocks)
    back = jnp.einsum("kim,bkm->kib", right_full, signal, precision=high)
    total = lax.psum(jnp.sum(spread * back, axis=(0, 1)), "blk")
    weight = scale / total
    returned = lax.all_to_all(back, "blk", split_axis=1, concat_axis=0, tiled=True)
    right_sum = jnp.einsum("kib,bkm->ikm", spread * weight, signal, precision=high)
    right_rows = lax.psum_scatter(right_sum, "seq", scatter_dimension=0, tiled=True)
    left_sum = jnp.einsum("kib,bij->kij", returned * weight, a_rows, precision=high)
    left_rows = lax.psum_scatter(left_sum, "seq", scatter_dimension=0, tiled=True)
    return (left_rows.transpose(1, 0, 2), right_rows.transpose(1, 0, 2))


def solution(mesh):
    placed = (
        P(None, "seq", "blk"),
        P(None, "seq", "blk"),
        P(None, "seq"),
        P(None, "blk"),
        P("blk", None, None),
        P("blk", "seq", None),
    )
    return jax.shard_map(
        local,
        mesh=mesh,
        in_specs=placed,
        out_specs=(P("blk", "seq", None), P("blk", "seq", None)),
        check_vma=False,
    )
```

```python
import functools
import jax
import jax.numpy as jnp
from jax import lax
from jax.experimental import pallas as pl
from jax.experimental.pallas import tpu as pltpu
from jax.sharding import PartitionSpec as P

F32 = jnp.float32
BF16 = jnp.bfloat16
CHIPS = 4
PARTS = 4
CHUNKS = 8


def halves(x):
    top = x.astype(BF16)
    rest = (x - top.astype(F32)).astype(BF16)
    return jnp.concatenate([top, rest], axis=0)


def loop(start, extent, body, unroll):
    def step(n, _):
        for v in range(unroll):
            body(start + n * unroll + v)
        return 0

    lax.fori_loop(0, extent // unroll, step, 0)


def nt(a, b):
    return lax.dot_general(a, b, (((1,), (1,)), ((), ())), preferred_element_type=F32)


def kernel(
    nz, scale, a_hbm, b_hbm, ids_ref, e_hbm, l_hbm, r_hbm, left_own, left_got, right_own, right_got,
    a32, b32, e32, l32, a16, g16, rf, us, ur, hs, hr, pr, pl_, rx0r, rx0l, rxar, rxal, rxbr, rxbl, cs, cr,
    load_a, load_l, load_b, load_e, load_r, own_u, own_h, ag_s, ag_r,
    u_s, u_r, h_s, h_r, c_s, c_r, s0_s, s0_r, s1_s, s1_r, s2_s, s2_r, own_g,
):
    seq = lax.axis_index("seq")
    z = lax.axis_index("blk")
    core, chip = seq % 2, seq // 2
    x, y = chip % 2, chip // 2
    sibling = 2 * chip + 1 - core
    across_x = 2 * (2 * y + 1 - x) + core
    across_y = 2 * (2 * (1 - y) + x) + core
    across = 2 * (2 * (1 - y) + 1 - x) + core
    blocks_here, window, width = l32.shape
    local_k, nblocks = g16.shape[0], g16.shape[2]
    count = a16.shape[1] // 2
    inputs = nz * blocks_here
    tokens = e32.shape[0]
    part_i, part_k = blocks_here // PARTS, local_k // PARTS
    rows_z = blocks_here * local_k
    rows_c = part_i * local_k

    loads_a, loads_l, loads_b, loads_e = [], [], [], []
    for n in range(PARTS):
        cols = pl.ds(n * part_i * width, part_i * width)
        loads_a.append(pltpu.make_async_copy(a_hbm.at[:, :, cols], a32.at[:, :, cols], load_a.at[n]))
        some = pl.ds(n * part_i, part_i)
        loads_l.append(pltpu.make_async_copy(l_hbm.at[some], l32.at[some], load_l.at[n]))
        cols = pl.ds(n * part_k * nblocks, part_k * nblocks)
        loads_b.append(pltpu.make_async_copy(b_hbm.at[:, :, cols], b32.at[:, :, cols], load_b.at[n]))
        loads_e.append(pltpu.make_async_copy(e_hbm.at[:, cols], e32.at[:, cols], load_e.at[n]))
    load_own = pltpu.make_async_copy(r_hbm, rf.at[seq], load_r)
    for n in range(PARTS):
        loads_l[n].start()
        loads_a[n].start()
    load_own.start()

    steps = (2, 3 - 2 * (z % 2), 1 + 2 * (z % 2)) if nz == 4 else tuple(range(1, nz))

    barrier = pltpu.get_barrier_semaphore()
    for other in (sibling, across_x, across_y):
        pl.semaphore_signal(barrier, inc=1, device_id={"seq": other}, device_id_type=pl.DeviceIdType.MESH)
    for d in range(1, nz):
        pl.semaphore_signal(barrier, inc=1, device_id={"blk": (z + d) % nz}, device_id_type=pl.DeviceIdType.MESH)

    def to_seq(src, dst, send, recv, other):
        return pltpu.make_async_remote_copy(
            src_ref=src, dst_ref=dst, send_sem=send, recv_sem=recv,
            device_id={"seq": other}, device_id_type=pl.DeviceIdType.MESH,
        )

    def to_blk(src, dst, send, recv, other):
        return pltpu.make_async_remote_copy(
            src_ref=src, dst_ref=dst, send_sem=send, recv_sem=recv,
            device_id={"blk": other}, device_id_type=pl.DeviceIdType.MESH,
        )

    started = []

    def gather(n, kind, owner, other, lo=0, size=local_k // PARTS, own=False):
        some = pl.ds(n * (local_k // PARTS) + lo, size)
        slot = rf.at[owner, some]
        copy = to_seq(r_hbm.at[some] if own else slot, slot, ag_s.at[kind, n], ag_r.at[kind, n], other)
        copy.start()
        started.append(copy)
        return copy

    gx, gy, gs, gd, fx, fy, fd = {}, {}, {}, {}, {}, {}, {}

    def near(n):
        half = part_k // 2
        gx[n].wait_recv()
        relay_y = gather(n, 3, across_x, across_y, 0, half)
        fx[n] = gather(n, 5, across_x, sibling)
        gy[n].wait_recv()
        relay_x = gather(n, 4, across_y, across_x, half, half)
        fy[n] = gather(n, 6, across_y, sibling)
        gd[n] = (relay_y, relay_x)

    def far(n):
        for copy in gd[n]:
            copy.wait_recv()
        fd[n] = gather(n, 7, across, sibling)

    def u_block(i):
        cols = pl.ds(pl.multiple_of(i * width, width), width)
        a = halves(jnp.concatenate([a32[0, :, cols], a32[1, :, cols]], axis=0))
        a16[i] = a
        both = nt(halves(l32[i]), a)
        u = both[:window, :count] + both[:window, count:] + both[window:, :count]
        for dz in range(nz):
            us[pl.ds(dz * rows_z + i * local_k, local_k), :] = u[dz * local_k:(dz + 1) * local_k]

    u_sends = []
    for n in range(PARTS):
        loads_l[n].wait()
        loads_a[n].wait()
        loop(n * part_i, part_i, u_block, 2)
        if n == 0:
            pl.semaphore_wait(barrier, 3 + nz - 1)
        for o, d in enumerate(steps):
            other = (z + d) % nz
            copy = to_blk(
                us.at[pl.ds(other * rows_z + n * rows_c, rows_c)],
                ur.at[pl.ds(z * rows_z + n * rows_c, rows_c)],
                u_s.at[n, o], u_r.at[n, o], other,
            )
            copy.start()
            u_sends.append(copy)
        if n == 0:
            for p in range(PARTS):
                gx[p] = gather(p, 0, seq, across_x, own=True)
                gy[p] = gather(p, 1, seq, across_y, own=True)
                gs[p] = gather(p, 2, seq, sibling, own=True)
        loads_e[n].start()
        loads_b[n].start()
    u_own = pltpu.make_async_copy(us.at[pl.ds(z * rows_z, rows_z)], ur.at[pl.ds(z * rows_z, rows_z)], own_u)
    u_own.start()

    token = lax.broadcasted_iota(jnp.int32, (128, count // 2), 0) % tokens
    hot = jnp.concatenate(
        [jnp.where(token == ids_ref[t:t + 1, :], 1.0, 0.0).astype(F32) for t in range(2)], axis=1
    )
    hot = jnp.transpose(hot)[:, :3 * tokens].astype(BF16)

    def g_block(k):
        cols = pl.ds(pl.multiple_of(k * nblocks, nblocks), nblocks)
        e = e32[:, cols]
        e1 = e.astype(BF16)
        rest = e - e1.astype(F32)
        e2 = rest.astype(BF16)
        e3 = (rest - e2.astype(F32)).astype(BF16)
        picked = jnp.dot(hot, jnp.concatenate([e1, e2, e3], axis=0), preferred_element_type=F32)
        b = jnp.concatenate([b32[0, :, cols], b32[1, :, cols]], axis=0)
        g16[k] = halves(picked * b)

    def h_block(k):
        r = halves(jnp.concatenate([rf[s, k] for s in range(2 * CHIPS)], axis=0))
        both = nt(r, g16[k])
        h = both[:inputs, :count] + both[:inputs, count:] + both[inputs:, :count]
        hs[pl.ds(k, inputs, stride=local_k), :] = h

    def h_part(n):
        if n == 0:
            load_own.wait()
        for copies in (gs, fx, fy, fd):
            copies[n].wait_recv()
        loop(n * part_k, part_k, h_block, 4)

    for n in range(PARTS):
        loads_e[n].wait()
        loads_b[n].wait()
        loop(n * part_k, part_k, g_block, 4)
        near(n)
        if n >= 1:
            far(n - 1)
        if n >= 2:
            h_part(n - 2)
    far(PARTS - 1)
    h_part(PARTS - 2)
    h_part(PARTS - 1)

    step = 64
    acc = jnp.zeros((8, count), F32)
    u_own.wait()
    for n in range(PARTS):
        for copy in u_sends[n * (nz - 1):(n + 1) * (nz - 1)]:
            copy.wait_recv()
        for sz in range(nz):
            for lo in range(0, rows_c, step):
                rows = pl.ds(sz * rows_z + n * rows_c + lo, step)
                acc = acc + jnp.sum((ur[rows, :] * hs[rows, :]).reshape(step // 8, 8, count), axis=0)
    cs[...] = acc
    c_sends = []
    for d in range(1, nz):
        copy = to_blk(cs, cr.at[d - 1], c_s.at[d - 1], c_r.at[d - 1], (z + d) % nz)
        copy.start()
        c_sends.append(copy)
    h_own = pltpu.make_async_copy(hs.at[pl.ds(z * rows_z, rows_z)], hr.at[pl.ds(z * rows_z, rows_z)], own_h)
    h_own.start()
    part_i, part_k = blocks_here // CHUNKS, local_k // CHUNKS
    rows_c = part_i * local_k
    h_sends = []
    for n in range(CHUNKS):
        for o, d in enumerate(steps):
            other = (z + d) % nz
            copy = to_blk(
                hs.at[pl.ds(other * rows_z + n * rows_c, rows_c)],
                hr.at[pl.ds(z * rows_z + n * rows_c, rows_c)],
                h_s.at[n, o], h_r.at[n, o], other,
            )
            copy.start()
            h_sends.append(copy)
    total = acc
    for n, copy in enumerate(c_sends):
        copy.wait_recv()
        total = total + cr[n]
    weight = scale / jnp.sum(total, axis=0, keepdims=True)

    def right_part(n):
        def block(kk):
            k = n * part_k + kk
            u = halves(ur[pl.ds(k, inputs, stride=local_k), :] * weight)
            both = jnp.dot(jnp.concatenate([u, u], axis=1), g16[k], preferred_element_type=F32)
            grad = both[:inputs] + both[inputs:]
            rows = inputs // (2 * CHIPS)
            for s in range(2 * CHIPS):
                pr[n, s % 2, s // 4, s // 2 % 2, kk] = grad[s * rows:(s + 1) * rows]

        loop(0, part_k, block, 4)

    def left_part(n):
        def block(ii):
            i = n * part_i + ii
            h = jnp.concatenate(
                [hr[pl.ds(pl.multiple_of(sz * rows_z + i * local_k, local_k), local_k), :] for sz in range(nz)], axis=0
            )
            h = halves(h * weight)
            both = jnp.dot(jnp.concatenate([h, h], axis=1), a16[i], preferred_element_type=F32)
            grad = both[:window] + both[window:]
            rows = window // (2 * CHIPS)
            for s in range(2 * CHIPS):
                pl_[n, s % 2, s // 4, s // 2 % 2, ii] = grad[s * rows:(s + 1) * rows]

        loop(0, part_i, block, 2)

    firsts, seconds, thirds, kept = {}, {}, {}, []

    def first(m):
        mine, rx0 = (pr, rx0r) if m < CHUNKS else (pl_, rx0l)
        n = m % CHUNKS
        firsts[m] = to_seq(mine.at[n, 1 - core], rx0.at[n], s0_s.at[m], s0_r.at[m], sibling)
        firsts[m].start()

    def second(m):
        mine, rx0, rxa, rxb = (pr, rx0r, rxar, rxbr) if m < CHUNKS else (pl_, rx0l, rxal, rxbl)
        n = m % CHUNKS
        half = mine.shape[4] // 2
        firsts[m].wait_recv()
        for p in range(2):
            for q in range(2):
                mine[n, core, p, q] = mine[n, core, p, q] + rx0[n, p, q]
        copy_x = to_seq(
            mine.at[n, core, :, 1 - x, pl.ds(0, half)], rxa.at[n], s1_s.at[m, 0], s1_r.at[m, 0], across_x
        )
        copy_y = to_seq(
            mine.at[n, core, 1 - y, :, pl.ds(half, half)], rxb.at[n], s1_s.at[m, 1], s1_r.at[m, 1], across_y
        )
        copy_x.start()
        copy_y.start()
        seconds[m] = (copy_x, copy_y)

    def third(m):
        mine, rxa, rxb, own, got = (
            (pr, rxar, rxbr, right_own, right_got) if m < CHUNKS else (pl_, rxal, rxbl, left_own, left_got)
        )
        n = m % CHUNKS
        part = mine.shape[4]
        half = part // 2
        low, top = pl.ds(0, half), pl.ds(half, half)
        seconds[m][0].wait_recv()
        mine[n, core, 1 - y, x, low] = mine[n, core, 1 - y, x, low] + rxa[n, 1 - y]
        copy_y = to_seq(
            mine.at[n, core, 1 - y, x, low], got.at[pl.ds(n * part, half)], s2_s.at[m, 0], s2_r.at[m, 0], across_y
        )
        copy_y.start()
        seconds[m][1].wait_recv()
        mine[n, core, y, 1 - x, top] = mine[n, core, y, 1 - x, top] + rxb[n, 1 - x]
        copy_x = to_seq(
            mine.at[n, core, y, 1 - x, top], got.at[pl.ds(n * part + half, half)], s2_s.at[m, 1], s2_r.at[m, 1], across_x
        )
        copy_x.start()
        thirds[m] = (copy_y, copy_x)
        mine[n, core, y, x, low] = mine[n, core, y, x, low] + rxa[n, y]
        mine[n, core, y, x, top] = mine[n, core, y, x, top] + rxb[n, x]
        keep = pltpu.make_async_copy(mine.at[n, core, y, x], own.at[pl.ds(n * part, part)], own_g.at[m])
        keep.start()
        kept.append(keep)

    last = 2 * CHUNKS
    for m in range(last + 3):
        n = m % CHUNKS
        if m < CHUNKS:
            right_part(n)
        elif m < last:
            if n == 0:
                h_own.wait()
            for copy in h_sends[n * (nz - 1):(n + 1) * (nz - 1)]:
                copy.wait_recv()
            left_part(n)
        if m < last:
            first(m)
        if 1 <= m <= last:
            second(m - 1)
        if m >= 3:
            third(m - 3)

    for copies in thirds.values():
        for copy in copies:
            copy.wait()
    for copy in kept:
        copy.wait()
    for copy in started + u_sends + c_sends + h_sends + list(firsts.values()):
        copy.wait_send()
    for copies in seconds.values():
        for copy in copies:
            copy.wait_send()


def last_sum(left_own, left_got, right_own, right_got, left, right):
    left[...] = left_own[...] + left_got[...]
    right[...] = right_own[...] + right_got[...]


def fused(alphas, betas, token_ids, emission, left_blocks, right_blocks):
    nz = lax.axis_size("blk")
    seq_dev = alphas.shape[1]
    count = 2 * seq_dev
    blocks_here, window, width = left_blocks.shape
    local_k, rows_right, nblocks = right_blocks.shape
    rows_left = window // (2 * CHIPS)
    scale = window * nblocks / (2.0 * seq_dev * lax.axis_size("seq"))
    part_i, part_k = blocks_here // CHUNKS, local_k // CHUNKS
    rows = nz * blocks_here * local_k
    dma = pltpu.SemaphoreType.DMA
    left_tile = (part_i, rows_left, width)
    right_tile = (part_k, rows_right, nblocks)
    left_half = (part_i // 2, rows_left, width)
    right_half = (part_k // 2, rows_right, nblocks)
    scratch = [
        pltpu.VMEM(alphas.shape, F32),
        pltpu.VMEM(betas.shape, F32),
        pltpu.VMEM(emission.shape, F32),
        pltpu.VMEM(left_blocks.shape, F32),
        pltpu.VMEM((blocks_here, 2 * count, width), BF16),
        pltpu.VMEM((local_k, 2 * count, nblocks), BF16),
        pltpu.VMEM((2 * CHIPS,) + right_blocks.shape, F32),
        pltpu.VMEM((rows, count), F32),
        pltpu.VMEM((rows, count), F32),
        pltpu.VMEM((rows, count), F32),
        pltpu.VMEM((rows, count), F32),
        pltpu.VMEM((CHUNKS, 2, 2, 2) + right_tile, F32),
        pltpu.VMEM((CHUNKS, 2, 2, 2) + left_tile, F32),
        pltpu.VMEM((CHUNKS, 2, 2) + right_tile, F32),
        pltpu.VMEM((CHUNKS, 2, 2) + left_tile, F32),
        pltpu.VMEM((CHUNKS, 2) + right_half, F32),
        pltpu.VMEM((CHUNKS, 2) + left_half, F32),
        pltpu.VMEM((CHUNKS, 2) + right_half, F32),
        pltpu.VMEM((CHUNKS, 2) + left_half, F32),
        pltpu.VMEM((8, count), F32),
        pltpu.VMEM((nz - 1, 8, count), F32),
        dma((PARTS,)), dma((PARTS,)), dma((PARTS,)), dma((PARTS,)), dma, dma, dma,
        dma((8, PARTS)), dma((8, PARTS)),
        dma((PARTS, nz - 1)), dma((PARTS, nz - 1)), dma((CHUNKS, nz - 1)), dma((CHUNKS, nz - 1)),
        dma((nz - 1,)), dma((nz - 1,)),
        dma((2 * CHUNKS,)), dma((2 * CHUNKS,)), dma((2 * CHUNKS, 2)), dma((2 * CHUNKS, 2)),
        dma((2 * CHUNKS, 2)), dma((2 * CHUNKS, 2)), dma((2 * CHUNKS,)),
    ]
    anywhere = pl.BlockSpec(memory_space=pl.ANY)
    vmem = pl.BlockSpec(memory_space=pltpu.VMEM)
    left_out = jax.ShapeDtypeStruct((blocks_here, rows_left, width), F32)
    right_out = jax.ShapeDtypeStruct(right_blocks.shape, F32)
    left_own, left_got, right_own, right_got = pl.pallas_call(
        functools.partial(kernel, nz, scale),
        out_shape=(left_out, left_out, right_out, right_out),
        in_specs=[anywhere, anywhere, vmem, anywhere, anywhere, anywhere],
        out_specs=(anywhere,) * 4,
        scratch_shapes=scratch,
        compiler_params=pltpu.CompilerParams(
            collective_id=0, has_side_effects=True, vmem_limit_bytes=60 * 2**20
        ),
        cost_estimate=pl.CostEstimate(flops=5 * 10**9, bytes_accessed=20 * 2**20, transcendentals=0),
    )(alphas, betas, token_ids, emission, left_blocks, right_blocks)
    flat = (-1, width)
    grid = 1
    left, right = pl.pallas_call(
        last_sum,
        grid=(grid,),
        out_shape=(
            jax.ShapeDtypeStruct((left_own.size // width, width), F32),
            jax.ShapeDtypeStruct((right_own.size // width, width), F32),
        ),
        in_specs=[
            pl.BlockSpec((part.size // width // grid, width), lambda n: (n, 0))
            for part in (left_own, left_got, right_own, right_got)
        ],
        out_specs=tuple(
            pl.BlockSpec((part.size // width // grid, width), lambda n: (n, 0)) for part in (left_own, right_own)
        ),
        compiler_params=pltpu.CompilerParams(vmem_limit_bytes=60 * 2**20),
    )(left_own.reshape(flat), left_got.reshape(flat), right_own.reshape(flat), right_got.reshape(flat))
    return left.reshape(left_own.shape), right.reshape(right_own.shape)


def local(alphas, betas, token_ids, emission, left_blocks, right_blocks):
    if (
        lax.axis_size("seq") == 2 * CHIPS
        and right_blocks.shape[0] % (4 * CHUNKS) == 0
        and right_blocks.shape[2] == left_blocks.shape[2]
        and right_blocks.shape[1] % 8 == 0
        and left_blocks.shape[0] % (2 * CHUNKS) == 0
        and 3 * emission.shape[0] <= 128
        and left_blocks.shape[1] % (16 * CHIPS) == 0
    ):
        return fused(alphas, betas, token_ids, emission, left_blocks, right_blocks)
    high = lax.Precision.HIGH
    seq_dev = alphas.shape[1]
    count = 2 * seq_dev
    blocks_here, window, width = left_blocks.shape
    local_k, rows_right, nblocks = right_blocks.shape
    scale = window * nblocks / (2.0 * seq_dev * lax.axis_size("seq"))

    right_full = lax.all_gather(right_blocks, "seq", axis=1, tiled=True)
    a_rows = alphas.reshape(count, blocks_here, width)
    mixed = jnp.einsum("ikj,bij->kib", left_blocks, a_rows, precision=high)
    spread = lax.all_to_all(mixed, "blk", split_axis=0, concat_axis=1, tiled=True)
    rows = jnp.take(emission, token_ids.reshape(count), axis=0)
    signal = (rows * betas.reshape(count, -1)).reshape(count, local_k, nblocks)
    back = jnp.einsum("kim,bkm->kib", right_full, signal, precision=high)
    total = lax.psum(jnp.sum(spread * back, axis=(0, 1)), "blk")
    weight = scale / total
    returned = lax.all_to_all(back, "blk", split_axis=1, concat_axis=0, tiled=True)
    right_sum = jnp.einsum("kib,bkm->ikm", spread * weight, signal, precision=high)
    right_rows = lax.psum_scatter(right_sum, "seq", scatter_dimension=0, tiled=True)
    left_sum = jnp.einsum("kib,bij->kij", returned * weight, a_rows, precision=high)
    left_rows = lax.psum_scatter(left_sum, "seq", scatter_dimension=0, tiled=True)
    return (left_rows.transpose(1, 0, 2), right_rows.transpose(1, 0, 2))


def solution(mesh):
    placed = (
        P(None, "seq", "blk"),
        P(None, "seq", "blk"),
        P(None, "seq"),
        P(None, "blk"),
        P("blk", None, None),
        P("blk", "seq", None),
    )
    return jax.shard_map(
        local,
        mesh=mesh,
        in_specs=placed,
        out_specs=(P("blk", "seq", None), P("blk", "seq", None)),
        check_vma=False,
    )
```

```python
import functools
import jax
import jax.numpy as jnp
from jax import lax
from jax.experimental import pallas as pl
from jax.experimental.pallas import tpu as pltpu
from jax.sharding import PartitionSpec as P

F32 = jnp.float32
BF16 = jnp.bfloat16
CHIPS = 4
PARTS = 4
CHUNKS = 8


def halves(x):
    top = x.astype(BF16)
    rest = (x - top.astype(F32)).astype(BF16)
    return jnp.concatenate([top, rest], axis=0)


def loop(start, extent, body, unroll):
    def step(n, _):
        for v in range(unroll):
            body(start + n * unroll + v)
        return 0

    lax.fori_loop(0, extent // unroll, step, 0)


def nt(a, b):
    return lax.dot_general(a, b, (((1,), (1,)), ((), ())), preferred_element_type=F32)


def kernel(
    nz, scale, a_hbm, b_hbm, ids_ref, e_hbm, l_hbm, r_hbm, left_own, left_got, right_own, right_got,
    a32, b32, e32, l32, a16, g16, rf, us, ur, hs, hr, pr, pl_, rx0r, rx0l, rxar, rxal, rxbr, rxbl, cs, cr,
    load_a, load_l, load_b, load_e, load_r, own_u, own_h, ag_s, ag_r,
    u_s, u_r, h_s, h_r, c_s, c_r, s0_s, s0_r, s1_s, s1_r, s2_s, s2_r, own_g,
):
    seq = lax.axis_index("seq")
    z = lax.axis_index("blk")
    core, chip = seq % 2, seq // 2
    x, y = chip % 2, chip // 2
    sibling = 2 * chip + 1 - core
    across_x = 2 * (2 * y + 1 - x) + core
    across_y = 2 * (2 * (1 - y) + x) + core
    across = 2 * (2 * (1 - y) + 1 - x) + core
    blocks_here, window, width = l32.shape
    local_k, nblocks = g16.shape[0], g16.shape[2]
    count = a16.shape[1] // 2
    inputs = nz * blocks_here
    tokens = e32.shape[0]
    part_i, part_k = blocks_here // PARTS, local_k // PARTS
    rows_z = blocks_here * local_k
    rows_c = part_i * local_k

    loads_a, loads_l, loads_b, loads_e = [], [], [], []
    for n in range(PARTS):
        cols = pl.ds(n * part_i * width, part_i * width)
        loads_a.append(pltpu.make_async_copy(a_hbm.at[:, :, cols], a32.at[:, :, cols], load_a.at[n]))
        some = pl.ds(n * part_i, part_i)
        loads_l.append(pltpu.make_async_copy(l_hbm.at[some], l32.at[some], load_l.at[n]))
        cols = pl.ds(n * part_k * nblocks, part_k * nblocks)
        loads_b.append(pltpu.make_async_copy(b_hbm.at[:, :, cols], b32.at[:, :, cols], load_b.at[n]))
        loads_e.append(pltpu.make_async_copy(e_hbm.at[:, cols], e32.at[:, cols], load_e.at[n]))
    load_own = pltpu.make_async_copy(r_hbm, rf.at[seq], load_r)
    for n in range(PARTS):
        loads_l[n].start()
        loads_a[n].start()
    load_own.start()
    for n in range(PARTS):
        loads_e[n].start()
        loads_b[n].start()

    steps = (2, 3 - 2 * (z % 2), 1 + 2 * (z % 2)) if nz == 4 else tuple(range(1, nz))

    barrier = pltpu.get_barrier_semaphore()
    for other in (sibling, across_x, across_y):
        pl.semaphore_signal(barrier, inc=1, device_id={"seq": other}, device_id_type=pl.DeviceIdType.MESH)
    for d in range(1, nz):
        pl.semaphore_signal(barrier, inc=1, device_id={"blk": (z + d) % nz}, device_id_type=pl.DeviceIdType.MESH)

    pl.semaphore_wait(barrier, 3 + nz - 1)

    def to_seq(src, dst, send, recv, other):
        return pltpu.make_async_remote_copy(
            src_ref=src, dst_ref=dst, send_sem=send, recv_sem=recv,
            device_id={"seq": other}, device_id_type=pl.DeviceIdType.MESH,
        )

    def to_blk(src, dst, send, recv, other):
        return pltpu.make_async_remote_copy(
            src_ref=src, dst_ref=dst, send_sem=send, recv_sem=recv,
            device_id={"blk": other}, device_id_type=pl.DeviceIdType.MESH,
        )

    started = []

    def gather(n, kind, owner, other, lo=0, size=local_k // PARTS, own=False):
        some = pl.ds(n * (local_k // PARTS) + lo, size)
        slot = rf.at[owner, some]
        copy = to_seq(r_hbm.at[some] if own else slot, slot, ag_s.at[kind, n], ag_r.at[kind, n], other)
        copy.start()
        started.append(copy)
        return copy

    gx, gy, gs, gd, fx, fy, fd = {}, {}, {}, {}, {}, {}, {}
    for n in range(PARTS):
        gx[n] = gather(n, 0, seq, across_x, own=True)
        gy[n] = gather(n, 1, seq, across_y, own=True)
        gs[n] = gather(n, 2, seq, sibling, own=True)

    def near(n):
        half = part_k // 2
        gx[n].wait_recv()
        relay_y = gather(n, 3, across_x, across_y, 0, half)
        fx[n] = gather(n, 5, across_x, sibling)
        gy[n].wait_recv()
        relay_x = gather(n, 4, across_y, across_x, half, half)
        fy[n] = gather(n, 6, across_y, sibling)
        gd[n] = (relay_y, relay_x)

    def far(n):
        for copy in gd[n]:
            copy.wait_recv()
        fd[n] = gather(n, 7, across, sibling)

    def u_block(i):
        cols = pl.ds(pl.multiple_of(i * width, width), width)
        a = halves(jnp.concatenate([a32[0, :, cols], a32[1, :, cols]], axis=0))
        a16[i] = a
        both = nt(halves(l32[i]), a)
        u = both[:window, :count] + both[:window, count:] + both[window:, :count]
        for dz in range(nz):
            us[pl.ds(dz * rows_z + i * local_k, local_k), :] = u[dz * local_k:(dz + 1) * local_k]

    u_sends = []
    for n in range(PARTS):
        loads_l[n].wait()
        loads_a[n].wait()
        loop(n * part_i, part_i, u_block, 2)
        for o, d in enumerate(steps):
            other = (z + d) % nz
            copy = to_blk(
                us.at[pl.ds(other * rows_z + n * rows_c, rows_c)],
                ur.at[pl.ds(z * rows_z + n * rows_c, rows_c)],
                u_s.at[n, o], u_r.at[n, o], other,
            )
            copy.start()
            u_sends.append(copy)
    u_own = pltpu.make_async_copy(us.at[pl.ds(z * rows_z, rows_z)], ur.at[pl.ds(z * rows_z, rows_z)], own_u)
    u_own.start()

    token = lax.broadcasted_iota(jnp.int32, (128, count // 2), 0) % tokens
    hot = jnp.concatenate(
        [jnp.where(token == ids_ref[t:t + 1, :], 1.0, 0.0).astype(F32) for t in range(2)], axis=1
    )
    hot = jnp.transpose(hot)[:, :3 * tokens].astype(BF16)

    def g_block(k):
        cols = pl.ds(pl.multiple_of(k * nblocks, nblocks), nblocks)
        e = e32[:, cols]
        e1 = e.astype(BF16)
        rest = e - e1.astype(F32)
        e2 = rest.astype(BF16)
        e3 = (rest - e2.astype(F32)).astype(BF16)
        picked = jnp.dot(hot, jnp.concatenate([e1, e2, e3], axis=0), preferred_element_type=F32)
        b = jnp.concatenate([b32[0, :, cols], b32[1, :, cols]], axis=0)
        g16[k] = halves(picked * b)

    def h_block(k):
        r = halves(jnp.concatenate([rf[s, k] for s in range(2 * CHIPS)], axis=0))
        both = nt(r, g16[k])
        h = both[:inputs, :count] + both[:inputs, count:] + both[inputs:, :count]
        hs[pl.ds(k, inputs, stride=local_k), :] = h

    def h_part(n):
        if n == 0:
            load_own.wait()
        for copies in (gs, fx, fy, fd):
            copies[n].wait_recv()
        loop(n * part_k, part_k, h_block, 4)

    for n in range(PARTS):
        loads_e[n].wait()
        loads_b[n].wait()
        loop(n * part_k, part_k, g_block, 4)
        near(n)
        if n >= 1:
            far(n - 1)
        if n >= 2:
            h_part(n - 2)
    far(PARTS - 1)
    h_part(PARTS - 2)
    h_part(PARTS - 1)

    step = 64
    acc = jnp.zeros((8, count), F32)
    u_own.wait()
    for n in range(PARTS):
        for copy in u_sends[n * (nz - 1):(n + 1) * (nz - 1)]:
            copy.wait_recv()
        for sz in range(nz):
            for lo in range(0, rows_c, step):
                rows = pl.ds(sz * rows_z + n * rows_c + lo, step)
                acc = acc + jnp.sum((ur[rows, :] * hs[rows, :]).reshape(step // 8, 8, count), axis=0)
    cs[...] = acc
    c_sends = []
    for d in range(1, nz):
        copy = to_blk(cs, cr.at[d - 1], c_s.at[d - 1], c_r.at[d - 1], (z + d) % nz)
        copy.start()
        c_sends.append(copy)
    h_own = pltpu.make_async_copy(hs.at[pl.ds(z * rows_z, rows_z)], hr.at[pl.ds(z * rows_z, rows_z)], own_h)
    h_own.start()
    part_i, part_k = blocks_here // CHUNKS, local_k // CHUNKS
    rows_c = part_i * local_k
    h_sends = []
    for n in range(CHUNKS):
        for o, d in enumerate(steps):
            other = (z + d) % nz
            copy = to_blk(
                hs.at[pl.ds(other * rows_z + n * rows_c, rows_c)],
                hr.at[pl.ds(z * rows_z + n * rows_c, rows_c)],
                h_s.at[n, o], h_r.at[n, o], other,
            )
            copy.start()
            h_sends.append(copy)
    total = acc
    for n, copy in enumerate(c_sends):
        copy.wait_recv()
        total = total + cr[n]
    weight = scale / jnp.sum(total, axis=0, keepdims=True)

    def right_part(n):
        def block(kk):
            k = n * part_k + kk
            u = halves(ur[pl.ds(k, inputs, stride=local_k), :] * weight)
            both = jnp.dot(jnp.concatenate([u, u], axis=1), g16[k], preferred_element_type=F32)
            grad = both[:inputs] + both[inputs:]
            rows = inputs // (2 * CHIPS)
            for s in range(2 * CHIPS):
                pr[n, s % 2, s // 4, s // 2 % 2, kk] = grad[s * rows:(s + 1) * rows]

        loop(0, part_k, block, 4)

    def left_part(n):
        def block(ii):
            i = n * part_i + ii
            h = jnp.concatenate(
                [hr[pl.ds(pl.multiple_of(sz * rows_z + i * local_k, local_k), local_k), :] for sz in range(nz)], axis=0
            )
            h = halves(h * weight)
            both = jnp.dot(jnp.concatenate([h, h], axis=1), a16[i], preferred_element_type=F32)
            grad = both[:window] + both[window:]
            rows = window // (2 * CHIPS)
            for s in range(2 * CHIPS):
                pl_[n, s % 2, s // 4, s // 2 % 2, ii] = grad[s * rows:(s + 1) * rows]

        loop(0, part_i, block, 2)

    firsts, seconds, thirds, kept = {}, {}, {}, []

    def first(m):
        mine, rx0 = (pr, rx0r) if m < CHUNKS else (pl_, rx0l)
        n = m % CHUNKS
        firsts[m] = to_seq(mine.at[n, 1 - core], rx0.at[n], s0_s.at[m], s0_r.at[m], sibling)
        firsts[m].start()

    def second(m):
        mine, rx0, rxa, rxb = (pr, rx0r, rxar, rxbr) if m < CHUNKS else (pl_, rx0l, rxal, rxbl)
        n = m % CHUNKS
        half = mine.shape[4] // 2
        firsts[m].wait_recv()
        for p in range(2):
            for q in range(2):
                mine[n, core, p, q] = mine[n, core, p, q] + rx0[n, p, q]
        copy_x = to_seq(
            mine.at[n, core, :, 1 - x, pl.ds(0, half)], rxa.at[n], s1_s.at[m, 0], s1_r.at[m, 0], across_x
        )
        copy_y = to_seq(
            mine.at[n, core, 1 - y, :, pl.ds(half, half)], rxb.at[n], s1_s.at[m, 1], s1_r.at[m, 1], across_y
        )
        copy_x.start()
        copy_y.start()
        seconds[m] = (copy_x, copy_y)

    def third(m):
        mine, rxa, rxb, own, got = (
            (pr, rxar, rxbr, right_own, right_got) if m < CHUNKS else (pl_, rxal, rxbl, left_own, left_got)
        )
        n = m % CHUNKS
        part = mine.shape[4]
        half = part // 2
        low, top = pl.ds(0, half), pl.ds(half, half)
        seconds[m][0].wait_recv()
        mine[n, core, 1 - y, x, low] = mine[n, core, 1 - y, x, low] + rxa[n, 1 - y]
        copy_y = to_seq(
            mine.at[n, core, 1 - y, x, low], got.at[pl.ds(n * part, half)], s2_s.at[m, 0], s2_r.at[m, 0], across_y
        )
        copy_y.start()
        seconds[m][1].wait_recv()
        mine[n, core, y, 1 - x, top] = mine[n, core, y, 1 - x, top] + rxb[n, 1 - x]
        copy_x = to_seq(
            mine.at[n, core, y, 1 - x, top], got.at[pl.ds(n * part + half, half)], s2_s.at[m, 1], s2_r.at[m, 1], across_x
        )
        copy_x.start()
        thirds[m] = (copy_y, copy_x)
        mine[n, core, y, x, low] = mine[n, core, y, x, low] + rxa[n, y]
        mine[n, core, y, x, top] = mine[n, core, y, x, top] + rxb[n, x]
        keep = pltpu.make_async_copy(mine.at[n, core, y, x], own.at[pl.ds(n * part, part)], own_g.at[m])
        keep.start()
        kept.append(keep)

    last = 2 * CHUNKS
    for m in range(last + 3):
        n = m % CHUNKS
        if m < CHUNKS:
            right_part(n)
        elif m < last:
            if n == 0:
                h_own.wait()
            for copy in h_sends[n * (nz - 1):(n + 1) * (nz - 1)]:
                copy.wait_recv()
            left_part(n)
        if m < last:
            first(m)
        if 1 <= m <= last:
            second(m - 1)
        if m >= 3:
            third(m - 3)

    for copies in thirds.values():
        for copy in copies:
            copy.wait()
    for copy in kept:
        copy.wait()
    for copy in started + u_sends + c_sends + h_sends + list(firsts.values()):
        copy.wait_send()
    for copies in seconds.values():
        for copy in copies:
            copy.wait_send()


def last_sum(left_own, left_got, right_own, right_got, left, right):
    left[...] = left_own[...] + left_got[...]
    right[...] = right_own[...] + right_got[...]


def fused(alphas, betas, token_ids, emission, left_blocks, right_blocks):
    nz = lax.axis_size("blk")
    seq_dev = alphas.shape[1]
    count = 2 * seq_dev
    blocks_here, window, width = left_blocks.shape
    local_k, rows_right, nblocks = right_blocks.shape
    rows_left = window // (2 * CHIPS)
    scale = window * nblocks / (2.0 * seq_dev * lax.axis_size("seq"))
    part_i, part_k = blocks_here // CHUNKS, local_k // CHUNKS
    rows = nz * blocks_here * local_k
    dma = pltpu.SemaphoreType.DMA
    left_tile = (part_i, rows_left, width)
    right_tile = (part_k, rows_right, nblocks)
    left_half = (part_i // 2, rows_left, width)
    right_half = (part_k // 2, rows_right, nblocks)
    scratch = [
        pltpu.VMEM(alphas.shape, F32),
        pltpu.VMEM(betas.shape, F32),
        pltpu.VMEM(emission.shape, F32),
        pltpu.VMEM(left_blocks.shape, F32),
        pltpu.VMEM((blocks_here, 2 * count, width), BF16),
        pltpu.VMEM((local_k, 2 * count, nblocks), BF16),
        pltpu.VMEM((2 * CHIPS,) + right_blocks.shape, F32),
        pltpu.VMEM((rows, count), F32),
        pltpu.VMEM((rows, count), F32),
        pltpu.VMEM((rows, count), F32),
        pltpu.VMEM((rows, count), F32),
        pltpu.VMEM((CHUNKS, 2, 2, 2) + right_tile, F32),
        pltpu.VMEM((CHUNKS, 2, 2, 2) + left_tile, F32),
        pltpu.VMEM((CHUNKS, 2, 2) + right_tile, F32),
        pltpu.VMEM((CHUNKS, 2, 2) + left_tile, F32),
        pltpu.VMEM((CHUNKS, 2) + right_half, F32),
        pltpu.VMEM((CHUNKS, 2) + left_half, F32),
        pltpu.VMEM((CHUNKS, 2) + right_half, F32),
        pltpu.VMEM((CHUNKS, 2) + left_half, F32),
        pltpu.VMEM((8, count), F32),
        pltpu.VMEM((nz - 1, 8, count), F32),
        dma((PARTS,)), dma((PARTS,)), dma((PARTS,)), dma((PARTS,)), dma, dma, dma,
        dma((8, PARTS)), dma((8, PARTS)),
        dma((PARTS, nz - 1)), dma((PARTS, nz - 1)), dma((CHUNKS, nz - 1)), dma((CHUNKS, nz - 1)),
        dma((nz - 1,)), dma((nz - 1,)),
        dma((2 * CHUNKS,)), dma((2 * CHUNKS,)), dma((2 * CHUNKS, 2)), dma((2 * CHUNKS, 2)),
        dma((2 * CHUNKS, 2)), dma((2 * CHUNKS, 2)), dma((2 * CHUNKS,)),
    ]
    anywhere = pl.BlockSpec(memory_space=pl.ANY)
    vmem = pl.BlockSpec(memory_space=pltpu.VMEM)
    left_out = jax.ShapeDtypeStruct((blocks_here, rows_left, width), F32)
    right_out = jax.ShapeDtypeStruct(right_blocks.shape, F32)
    left_own, left_got, right_own, right_got = pl.pallas_call(
        functools.partial(kernel, nz, scale),
        out_shape=(left_out, left_out, right_out, right_out),
        in_specs=[anywhere, anywhere, vmem, anywhere, anywhere, anywhere],
        out_specs=(anywhere,) * 4,
        scratch_shapes=scratch,
        compiler_params=pltpu.CompilerParams(
            collective_id=0, has_side_effects=True, vmem_limit_bytes=60 * 2**20
        ),
        cost_estimate=pl.CostEstimate(flops=5 * 10**9, bytes_accessed=20 * 2**20, transcendentals=0),
    )(alphas, betas, token_ids, emission, left_blocks, right_blocks)
    flat = (-1, width)
    grid = 1
    left, right = pl.pallas_call(
        last_sum,
        grid=(grid,),
        out_shape=(
            jax.ShapeDtypeStruct((left_own.size // width, width), F32),
            jax.ShapeDtypeStruct((right_own.size // width, width), F32),
        ),
        in_specs=[
            pl.BlockSpec((part.size // width // grid, width), lambda n: (n, 0))
            for part in (left_own, left_got, right_own, right_got)
        ],
        out_specs=tuple(
            pl.BlockSpec((part.size // width // grid, width), lambda n: (n, 0)) for part in (left_own, right_own)
        ),
        compiler_params=pltpu.CompilerParams(vmem_limit_bytes=60 * 2**20),
    )(left_own.reshape(flat), left_got.reshape(flat), right_own.reshape(flat), right_got.reshape(flat))
    return left.reshape(left_own.shape), right.reshape(right_own.shape)


def local(alphas, betas, token_ids, emission, left_blocks, right_blocks):
    if (
        lax.axis_size("seq") == 2 * CHIPS
        and right_blocks.shape[0] % (4 * CHUNKS) == 0
        and right_blocks.shape[2] == left_blocks.shape[2]
        and right_blocks.shape[1] % 8 == 0
        and left_blocks.shape[0] % (2 * CHUNKS) == 0
        and 3 * emission.shape[0] <= 128
        and left_blocks.shape[1] % (16 * CHIPS) == 0
    ):
        return fused(alphas, betas, token_ids, emission, left_blocks, right_blocks)
    high = lax.Precision.HIGH
    seq_dev = alphas.shape[1]
    count = 2 * seq_dev
    blocks_here, window, width = left_blocks.shape
    local_k, rows_right, nblocks = right_blocks.shape
    scale = window * nblocks / (2.0 * seq_dev * lax.axis_size("seq"))

    right_full = lax.all_gather(right_blocks, "seq", axis=1, tiled=True)
    a_rows = alphas.reshape(count, blocks_here, width)
    mixed = jnp.einsum("ikj,bij->kib", left_blocks, a_rows, precision=high)
    spread = lax.all_to_all(mixed, "blk", split_axis=0, concat_axis=1, tiled=True)
    rows = jnp.take(emission, token_ids.reshape(count), axis=0)
    signal = (rows * betas.reshape(count, -1)).reshape(count, local_k, nblocks)
    back = jnp.einsum("kim,bkm->kib", right_full, signal, precision=high)
    total = lax.psum(jnp.sum(spread * back, axis=(0, 1)), "blk")
    weight = scale / total
    returned = lax.all_to_all(back, "blk", split_axis=1, concat_axis=0, tiled=True)
    right_sum = jnp.einsum("kib,bkm->ikm", spread * weight, signal, precision=high)
    right_rows = lax.psum_scatter(right_sum, "seq", scatter_dimension=0, tiled=True)
    left_sum = jnp.einsum("kib,bij->kij", returned * weight, a_rows, precision=high)
    left_rows = lax.psum_scatter(left_sum, "seq", scatter_dimension=0, tiled=True)
    return (left_rows.transpose(1, 0, 2), right_rows.transpose(1, 0, 2))


def solution(mesh):
    placed = (
        P(None, "seq", "blk"),
        P(None, "seq", "blk"),
        P(None, "seq"),
        P(None, "blk"),
        P("blk", None, None),
        P("blk", "seq", None),
    )
    return jax.shard_map(
        local,
        mesh=mesh,
        in_specs=placed,
        out_specs=(P("blk", "seq", None), P("blk", "seq", None)),
        check_vma=False,
    )
```
